256 devices in a mesh: member: 32 (over x, y, core), space: 8 (over z).
Axes of the slice: x: 4, y: 4, z: 8, core: 2. Of those that a mesh axis runs over, the one named last changes fastest.
Arguments:
- realization_fields: float32 [32, 4, 16, 16384], P('member', None, 'space'), may hold values from -6 to 6
- viscosity: float32 [16, 16384], P('space'), may hold values from 0.01 to 0.08
- cell_index: int32 [8, 65536], P('space'), may hold values from 0 to 1023
- beam_id: int32 [8, 65536], P('space'), may hold values from 0 to 16383
- los_weight: float32 [8, 3, 65536], P('space'), may hold values from -0.625 to 0.625
- observed: float32 [16384], replicated, may hold values from -16 to 16
- obs_variance: float32 [16384], replicated, may hold values from 64 to 256
Outputs:
- analysis: float32 [32, 4, 16, 16384], P('member', None, 'space')
- mixing: float32 [32, 32], replicated
The draws below stay inside these ranges and needn't reach their ends.
All inputs are finite; a program needn't handle non-finite values.
Results may differ from the reference program's by a relative error of at most 0.00014.
Values sent between devices are 32-bit elements; how exact they have to be, the bound alone decides.
A program may use at most 192 MiB of HBM per device.

```python
import math
import jax
import jax.numpy as jnp
from jax import lax

ENSEMBLE_SIZE = 32
CELLS_FIRST_DIM = 2
CELLS_SECOND_DIM = 256
CELLS_THIRD_DIM = 64
SAMP_PIECE = 2048
NOBS = 16384
NS_STEPS = 8
NX = 16
PIECE = 1024
SAMPLES = 65536
SAMP_BEAM = 32
N_MEMBER = 32
N_SPACE = 8


def set_ends(values, key, least, top_value):
    longest = values.shape.index(max(values.shape))
    spots = []
    for shift in (0, 1):
        where = [jax.random.randint(jax.random.fold_in(key, axis), (), 0, length) for axis, length in enumerate(values.shape)]
        where[longest] = (where[longest] + shift) % values.shape[longest]
        spots.append(tuple(where))
    return values.at[spots[0]].set(least).at[spots[1]].set(top_value)


def block_levels(own_key, dims, shards, low, top_value):
    def one(dim, shards_of):
        draws = jax.random.uniform(jax.random.fold_in(jax.random.fold_in(own_key, 6), dim), (shards_of,), jnp.float32, low / len(shards), top_value / len(shards))
        return jnp.repeat(jnp.exp(draws), dims[dim] // shards_of).reshape((-1,) + (1,) * (len(dims) - dim - 1))

    factor_of = one(*shards[0])
    for cut in shards[1:]:
        factor_of = factor_of * one(*cut)
    return factor_of


def bell_draw(stream_key, dims, scale, limit, split=(), kind=jnp.bfloat16):
    loudness = block_levels(stream_key, dims, split, -0.22, 0.18) if split else 1.0
    entries = jax.random.normal(stream_key, dims, jnp.float32) * scale * loudness
    return jnp.minimum(jnp.maximum(entries, -limit), limit).astype(kind)


def setup_inputs(seed: int = 0) -> dict:
    arg_keys = jax.random.split(jax.random.key(seed), 8)
    realization_fields = bell_draw(arg_keys[0], (ENSEMBLE_SIZE, 4, NX, CELLS_SECOND_DIM * CELLS_THIRD_DIM), 1.0, 6.0, ((0, 32), (2, 8)), jnp.float32)
    viscosity = jnp.clip(jnp.exp(math.log(0.08) - 2.0794415 * jax.random.uniform(arg_keys[1], (NX, CELLS_SECOND_DIM * CELLS_THIRD_DIM), jnp.float32) ** block_levels(arg_keys[1], (NX, CELLS_SECOND_DIM * CELLS_THIRD_DIM), ((0, 8),), -0.2, 0.2)), 0.01, 0.08)
    cell_index = set_ends(jax.random.randint(arg_keys[2], (N_SPACE, SAMPLES), 0, PIECE), jax.random.fold_in(arg_keys[2], 1), 0, PIECE - 1).astype(jnp.int32)
    beam_id = set_ends(jax.random.randint(arg_keys[3], (N_SPACE, SAMPLES), 0, NOBS), jax.random.fold_in(arg_keys[3], 1), 0, NOBS - 1).astype(jnp.int32)
    los_weight = bell_draw(arg_keys[4], (N_SPACE, 3, SAMPLES), (3 * SAMP_BEAM) ** -0.5, 0.625, ((0, 8),), jnp.float32)
    observed = bell_draw(arg_keys[5], (NOBS,), 4.0, 16.0, (), jnp.float32)
    obs_variance = jnp.clip(jnp.exp(jax.random.uniform(arg_keys[6], (NOBS,), jnp.float32, math.log(64.0), math.log(256.0))), 64.0, 256.0)
    return dict(realization_fields=realization_fields, viscosity=viscosity, cell_index=cell_index, beam_id=beam_id, los_weight=los_weight, observed=observed, obs_variance=obs_variance)


COURANT = 0.5
BUOYANCY = 0.2

def advance(extended, viscosity):
    count = extended.shape[2] - 2
    members = extended.shape[0]
    shaped = extended.reshape(members, 4, count + 2, CELLS_SECOND_DIM, CELLS_THIRD_DIM)
    center = shaped[:, :, 1:-1]
    behind = shaped[:, :, :-2]
    ahead = shaped[:, :, 2:]
    lateral = jnp.roll(center, 1, axis=3) + jnp.roll(center, -1, axis=3)
    bordered_field = jnp.pad(center, ((0, 0), (0, 0), (0, 0), (0, 0), (1, 1)))
    vertical = bordered_field[..., 2:] + bordered_field[..., :-2]
    laplace = behind + ahead + lateral + vertical - 6.0 * center
    viscous = viscosity.reshape(count, CELLS_SECOND_DIM, CELLS_THIRD_DIM)
    moved = center - COURANT * (center - behind) + viscous * laplace
    lifted = moved[:, 2] + BUOYANCY * center[:, 3]
    cooled = moved[:, 3] - BUOYANCY * center[:, 2]
    result = jnp.stack([moved[:, 0], moved[:, 1], lifted, cooled], axis=1)
    return result.reshape(members, 4, count, CELLS_SECOND_DIM * CELLS_THIRD_DIM)

def innovation_stats(predicted, observed, obs_variance):
    mean_pred = lax.optimization_barrier(jnp.mean(predicted, axis=0))
    anomaly = predicted - mean_pred[None]
    scaled = anomaly / obs_variance[None]
    covar = jnp.dot(scaled, anomaly.T, precision=lax.Precision.HIGHEST)
    drive = jnp.dot(scaled, observed - mean_pred, precision=lax.Precision.HIGHEST)
    return (covar, drive)

def ensemble_transform(covar, drive):
    count = covar.shape[0]
    identity = jnp.eye(count, dtype=jnp.float32)
    system = identity + covar / (count - 1.0)
    magnitude = jnp.sqrt(jnp.sum(system * system))
    iterate = system / magnitude
    inverse_root = identity
    for sweep_index in range(NS_STEPS):
        factor = 1.5 * identity - 0.5 * jnp.dot(inverse_root, iterate, precision=lax.Precision.HIGHEST)
        iterate = jnp.dot(iterate, factor, precision=lax.Precision.HIGHEST)
        inverse_root = jnp.dot(factor, inverse_root, precision=lax.Precision.HIGHEST)
    root_part = inverse_root / jnp.sqrt(magnitude)
    inverse_full = jnp.dot(inverse_root, inverse_root, precision=lax.Precision.HIGHEST) / magnitude
    shift = jnp.dot(inverse_full, drive, precision=lax.Precision.HIGHEST) / (count - 1.0)
    combined = root_part + shift[:, None]
    return combined - lax.optimization_barrier(jnp.mean(combined, axis=0, keepdims=True)) + 1.0 / count

def reference(realization_fields, viscosity, cell_index, beam_id, los_weight, observed, obs_variance):

    def upfront_prediction(realization_number):
        present_guess = realization_number[None]
        for sweep_index in range(2):
            extended = jnp.concatenate([present_guess[:, :, -1:], present_guess, present_guess[:, :, :1]], axis=2)
            present_guess = advance(extended, viscosity)
        return present_guess[0]
    upfront_realization_fields = lax.map(upfront_prediction, realization_fields)
    flattened = upfront_realization_fields.reshape(ENSEMBLE_SIZE, 4, N_SPACE, CELLS_FIRST_DIM * CELLS_SECOND_DIM * CELLS_THIRD_DIM)
    piece_len = CELLS_FIRST_DIM * CELLS_SECOND_DIM * CELLS_THIRD_DIM // N_MEMBER
    positions = jnp.arange(N_MEMBER * SAMP_PIECE, dtype=jnp.int32)
    slab_cells = (positions // SAMP_PIECE)[None, :] * piece_len + cell_index
    predicted = jnp.zeros((ENSEMBLE_SIZE, NOBS), jnp.float32)
    for slab_index in range(N_SPACE):
        values = jnp.take(flattened[:, :3, slab_index], slab_cells[slab_index], axis=2)
        sightline = lax.optimization_barrier(jnp.sum(values * los_weight[slab_index][None], axis=1))
        predicted = predicted + jax.ops.segment_sum(sightline.T, beam_id[slab_index], num_segments=NOBS).T
    covar, drive = innovation_stats(predicted, observed, obs_variance)
    mixing = ensemble_transform(covar, drive)
    analysis = jnp.einsum('gh,gubo->hubo', mixing, upfront_realization_fields, precision=lax.Precision.HIGHEST)
    return (analysis, mixing)
```

```python
import functools

import jax
import jax.numpy as jnp
from jax import lax
from jax.experimental import pallas as pl
from jax.experimental.pallas import tpu as pltpu
from jax.sharding import PartitionSpec as P

NS_STEPS = 8
COURANT = 0.5
BUOYANCY = 0.2
FIELDS = 4
LANES = 128
HALF = 64
BEAM_ROWS = 64
BEAM_COLS = 256
PARTS = 3
ORDER = (2, 3, 0, 1)
MESH = pl.DeviceIdType.MESH
F32 = jnp.float32
BF16 = jnp.bfloat16
HIGHEST = lax.Precision.HIGHEST


def bf16_iota(shape, dim):
    return lax.broadcasted_iota(jnp.int32, shape, dim).astype(F32).astype(BF16)


def stencil(center, behind, ahead, viscous):
    lane = lax.broadcasted_iota(jnp.int32, center.shape, 1)
    depth = lane & (HALF - 1)
    rows = center.shape[0]
    swapped = pltpu.roll(center, HALF, 1)
    lateral = swapped + jnp.where(
        lane < HALF, pltpu.roll(swapped, 1, 0), pltpu.roll(swapped, rows - 1, 0)
    )
    above = jnp.where(depth == HALF - 1, 0.0, pltpu.roll(center, LANES - 1, 1))
    below = jnp.where(depth == 0, 0.0, pltpu.roll(center, 1, 1))
    laplace = behind + ahead + lateral + (above + below) - 6.0 * center
    return center - COURANT * (center - behind) + viscous * laplace


def kernel(
    members, spaces,
    fields_ref, visc_ref, cell_ref, beam_ref, weight_ref, observed_ref, variance_ref,
    out_ref, mixing_ref,
    planes, visc, halo_low, halo_high, forecast, pointwise, sight, scatter,
    beam_send, beam_recv, gathered, stats_send, stats_recv, mixed, returned,
    halo_send_sem, halo_recv_sem, there_send_sem, there_recv_sem, beam_send_sem, beam_recv_sem,
    gather_send_sem, gather_recv_sem, stats_send_sem, stats_recv_sem, back_send_sem, back_recv_sem,
):
    me = lax.axis_index("member")
    here = lax.axis_index("space")
    nxt = lax.rem(here + 1, spaces)
    prv = lax.rem(here + spaces - 1, spaces)

    barrier = pltpu.get_barrier_semaphore()

    def greet_space(d, carry):
        pl.semaphore_signal(
            barrier, inc=1, device_id=(me, lax.rem(here + d, spaces)), device_id_type=MESH
        )
        return carry

    def greet_member(d, carry):
        pl.semaphore_signal(
            barrier, inc=1, device_id=(lax.rem(me + d, members), here), device_id_type=MESH
        )
        return carry

    lax.fori_loop(1, spaces, greet_space, 0)
    lax.fori_loop(1, members, greet_member, 0)
    pl.semaphore_wait(barrier, members + spaces - 2)

    def halo_copies(step, f):
        base = (step * FIELDS + f) * 2
        down = pltpu.make_async_remote_copy(
            src_ref=planes.at[step, 0, f], dst_ref=halo_high.at[step, f],
            send_sem=halo_send_sem.at[base], recv_sem=halo_recv_sem.at[base],
            device_id=(me, prv), device_id_type=MESH,
        )
        up = pltpu.make_async_remote_copy(
            src_ref=planes.at[step, 1, f], dst_ref=halo_low.at[step, f],
            send_sem=halo_send_sem.at[base + 1], recv_sem=halo_recv_sem.at[base + 1],
            device_id=(me, nxt), device_id_type=MESH,
        )
        return down, up

    def start_halo(step, f):
        for copy in halo_copies(step, f):
            copy.start()

    def finish_halo(step, f):
        for copy in halo_copies(step, f):
            copy.wait()

    for f in ORDER:
        for r in range(2):
            planes[0, r, f] = fields_ref[f, pl.ds(r, LANES, stride=2), :]
        start_halo(0, f)
    for r in range(2):
        visc[r] = visc_ref[pl.ds(r, LANES, stride=2), :]

    def advance(step, group):
        for f in group:
            finish_halo(step, f)
        for r in range(2):
            moved = []
            for f in group:
                center = planes[step, r, f]
                behind = halo_low[step, f] if r == 0 else planes[step, 0, f]
                ahead = planes[step, 1, f] if r == 0 else halo_high[step, f]
                moved.append(stencil(center, behind, ahead, visc[r]))
            if len(group) == 2:
                moved[0] = moved[0] + BUOYANCY * planes[step, r, group[1]]
                moved[1] = moved[1] - BUOYANCY * planes[step, r, group[0]]
            for f, value in zip(group, moved):
                if step == 0:
                    planes[1, r, f] = value
                else:
                    blocks = members // 2
                    forecast[pl.ds(r * blocks, blocks), f] = value.reshape(blocks, 8, LANES)

    groups = ((2, 3), (0,), (1,))
    for group in groups:
        advance(0, group)
        for f in group:
            start_halo(1, f)
    for group in groups:
        advance(1, group)

    def there(p):
        return pltpu.make_async_remote_copy(
            src_ref=forecast.at[p], dst_ref=pointwise.at[me],
            send_sem=there_send_sem.at[p], recv_sem=there_recv_sem.at[me],
            device_id=(p, here), device_id_type=MESH,
        )

    def there_from(i):
        return pltpu.make_async_remote_copy(
            src_ref=forecast.at[i], dst_ref=pointwise.at[i],
            send_sem=there_send_sem.at[i], recv_sem=there_recv_sem.at[i],
            device_id=(i, here), device_id_type=MESH,
        )

    def others(count, mine, act):
        def one(d, carry):
            act(lax.rem(mine + d, count))
            return carry

        lax.fori_loop(1, count, one, 0)

    others(members, me, lambda p: there(p).start())
    pointwise[me] = forecast[me]

    def gather_block(p):
        for g in range(2):
            rows = pl.ds(pl.multiple_of(16 * p + 8 * g, 8), 8)
            cells = cell_ref[rows, :]
            low, high = cells & (LANES - 1), cells >> 7
            total = None
            for c in range(3):
                table = forecast[p, c]
                value = None
                for t in range(8):
                    row = jnp.broadcast_to(table[t : t + 1], (8, LANES))
                    found = jnp.take_along_axis(row, low, axis=1, mode="promise_in_bounds")
                    value = found if value is None else jnp.where(high == t, found, value)
                term = weight_ref[c, rows, :] * value
                total = term if total is None else total + term
            sight[rows, :] = total

    def scatter_block(p):
        rows = pl.ds(pl.multiple_of(16 * p, 16), 16)
        rest = sight[rows, :]
        beams = beam_ref[rows, :]
        parts = []
        for _ in range(PARTS):
            part = rest.astype(BF16)
            parts.append(part)
            rest = rest - part.astype(F32)
        beam_row = (beams >> 8).astype(F32).astype(BF16)
        beam_col = (beams & (BEAM_COLS - 1)).astype(F32).astype(BF16)
        col_ids = bf16_iota((BEAM_COLS, LANES), 0)
        row_ids = bf16_iota((BEAM_ROWS, LANES), 0)
        ones, zeros = jnp.ones((BEAM_COLS, LANES), BF16), jnp.zeros((BEAM_COLS, LANES), BF16)
        left, right = [], []
        for g in range(16):
            right.append(jnp.where(col_ids == beam_col[g : g + 1], ones, zeros))
            hit = row_ids == beam_row[g : g + 1]
            left.append(jnp.concatenate([
                jnp.where(hit, jnp.broadcast_to(part[g : g + 1], (BEAM_ROWS, LANES)), zeros[:BEAM_ROWS])
                for part in parts
            ], axis=0))
        scatter[...] += lax.dot_general(
            jnp.concatenate(left, axis=1), jnp.concatenate(right, axis=1),
            (((1,), (1,)), ((), ())), preferred_element_type=F32,
        )

    scatter[...] = jnp.zeros_like(scatter)
    gather_block(0)

    def samples(p, carry):
        scatter_block(p - 1)
        gather_block(p)
        return carry

    lax.fori_loop(1, members, samples, 0)
    scatter_block(members - 1)
    total = scatter[0:BEAM_ROWS]
    for i in range(1, PARTS):
        total = total + scatter[BEAM_ROWS * i : BEAM_ROWS * (i + 1)]
    beam_send[...] = total.reshape(beam_send.shape)

    def beam_to(t):
        return pltpu.make_async_remote_copy(
            src_ref=beam_send.at[t], dst_ref=beam_recv.at[here],
            send_sem=beam_send_sem.at[t], recv_sem=beam_recv_sem.at[here],
            device_id=(me, t), device_id_type=MESH,
        )

    def beam_from(t):
        return pltpu.make_async_remote_copy(
            src_ref=beam_send.at[t], dst_ref=beam_recv.at[t],
            send_sem=beam_send_sem.at[t], recv_sem=beam_recv_sem.at[t],
            device_id=(me, t), device_id_type=MESH,
        )

    others(spaces, here, lambda t: beam_to(t).start())
    beam_recv[here] = beam_send[here]
    others(spaces, here, lambda t: beam_from(t).wait_recv())
    predicted = beam_recv[0]
    for t in range(1, spaces):
        predicted = predicted + beam_recv[t]

    def slot(i):
        return gathered.at[pl.ds(pl.multiple_of(16 * i, 16), 16), :]

    def share_to(p):
        return pltpu.make_async_remote_copy(
            src_ref=slot(me), dst_ref=slot(me),
            send_sem=gather_send_sem.at[p], recv_sem=gather_recv_sem.at[me],
            device_id=(p, here), device_id_type=MESH,
        )

    def share_from(i):
        return pltpu.make_async_remote_copy(
            src_ref=slot(i), dst_ref=slot(i),
            send_sem=gather_send_sem.at[i], recv_sem=gather_recv_sem.at[i],
            device_id=(i, here), device_id_type=MESH,
        )

    for half in range(2):
        gathered[pl.ds(pl.multiple_of(16 * me + 8 * half, 8), 8), :] = (
            predicted[:, half * LANES : (half + 1) * LANES]
        )
    others(members, me, lambda p: share_to(p).start())
    others(members, me, lambda i: share_from(i).wait_recv())

    every = jnp.concatenate(
        [
            gathered[pl.ds(8 * half + sub, members, stride=16), :]
            for sub in range(8) for half in range(2)
        ],
        axis=1,
    )
    mine = pl.ds(pl.multiple_of(16 * here, 16), 16)
    seen_rows, var_rows = observed_ref[mine, :], variance_ref[mine, :]
    seen = jnp.concatenate([seen_rows[i : i + 1] for i in range(16)], axis=1)
    variance = jnp.concatenate([var_rows[i : i + 1] for i in range(16)], axis=1)
    mean_pred = jnp.mean(every, axis=0, keepdims=True)
    anomaly = every - mean_pred
    scaled = anomaly / variance
    width = anomaly.shape[1]
    against = jnp.concatenate(
        [anomaly, seen - mean_pred, jnp.zeros((LANES - members - 1, width), F32)], axis=0
    )
    stats_send[...] = lax.dot_general(
        scaled, against, (((1,), (1,)), ((), ())), precision=HIGHEST, preferred_element_type=F32
    )

    def stats_to(t):
        return pltpu.make_async_remote_copy(
            src_ref=stats_send, dst_ref=stats_recv.at[here],
            send_sem=stats_send_sem.at[t], recv_sem=stats_recv_sem.at[here],
            device_id=(me, t), device_id_type=MESH,
        )

    def stats_from(t):
        return pltpu.make_async_remote_copy(
            src_ref=stats_send, dst_ref=stats_recv.at[t],
            send_sem=stats_send_sem.at[t], recv_sem=stats_recv_sem.at[t],
            device_id=(me, t), device_id_type=MESH,
        )

    others(spaces, here, lambda t: stats_to(t).start())
    stats_recv[here] = stats_send[...]
    others(spaces, here, lambda t: stats_from(t).wait_recv())
    stats = stats_recv[0]
    for t in range(1, spaces):
        stats = stats + stats_recv[t]

    def times(a, b):
        return jnp.dot(a, b, precision=HIGHEST, preferred_element_type=F32)

    covar = stats[:, :members]
    row_id = lax.broadcasted_iota(jnp.int32, (members, members), 0)
    col_id = lax.broadcasted_iota(jnp.int32, (members, members), 1)
    identity = jnp.where(row_id == col_id, 1.0, 0.0).astype(F32)
    system = identity + covar / (members - 1.0)
    magnitude = jnp.sqrt(jnp.sum(system * system, axis=(0, 1), keepdims=True))
    iterate = system / magnitude
    inverse_root = identity
    for _ in range(NS_STEPS):
        factor = 1.5 * identity - 0.5 * times(inverse_root, iterate)
        iterate = times(iterate, factor)
        inverse_root = times(factor, inverse_root)
    root_part = inverse_root / jnp.sqrt(magnitude)
    inverse_full = times(inverse_root, inverse_root) / magnitude
    shift = times(inverse_full, stats)[:, members : members + 1] / (members - 1.0)
    combined = root_part + shift
    mixing = combined - jnp.mean(combined, axis=0, keepdims=True) + 1.0 / members
    mixing_ref[...] = mixing

    others(members, me, lambda i: there_from(i).wait_recv())
    count = FIELDS * 8
    block = jnp.concatenate(
        [pointwise.reshape(members * count, LANES)[pl.ds(k, members, stride=count), :] for k in range(count)],
        axis=1,
    )
    analysed = lax.dot_general(
        mixing, block, (((0,), (0,)), ((), ())), precision=HIGHEST, preferred_element_type=F32
    )
    for k in range(count):
        mixed.reshape(members * count, LANES)[pl.ds(k, members, stride=count), :] = (
            analysed[:, k * LANES : (k + 1) * LANES]
        )

    def back(j):
        return pltpu.make_async_remote_copy(
            src_ref=mixed.at[j], dst_ref=returned.at[me],
            send_sem=back_send_sem.at[j], recv_sem=back_recv_sem.at[me],
            device_id=(j, here), device_id_type=MESH,
        )

    def back_from(p):
        return pltpu.make_async_remote_copy(
            src_ref=mixed.at[p], dst_ref=returned.at[p],
            send_sem=back_send_sem.at[p], recv_sem=back_recv_sem.at[p],
            device_id=(p, here), device_id_type=MESH,
        )

    others(members, me, lambda j: back(j).start())
    returned[me] = mixed[me]
    others(members, me, lambda p: there(p).wait_send())
    others(spaces, here, lambda t: beam_to(t).wait_send())
    others(members, me, lambda p: share_to(p).wait_send())
    others(spaces, here, lambda t: stats_to(t).wait_send())
    others(members, me, lambda p: back_from(p).wait_recv())
    for p in range(members):
        r, q = divmod(p, members // 2)
        for f in range(FIELDS):
            out_ref[f, pl.ds(16 * q + r, 8, stride=2), :] = returned[p, f]
    others(members, me, lambda j: back(j).wait_send())


def shards(members, spaces, realization_fields, viscosity, cell_index, beam_id, los_weight, observed, obs_variance):
    _, fields, rows, plane = realization_fields.shape
    lines = plane // LANES
    samples = cell_index.shape[1] // LANES
    beams = observed.shape[0] // LANES
    mixed_rows = realization_fields.reshape(fields, rows, lines, LANES).transpose(0, 2, 1, 3)
    visc_rows = viscosity.reshape(rows, lines, LANES).transpose(1, 0, 2)
    block = (members, FIELDS, 8, LANES)
    share = (BEAM_ROWS // spaces, BEAM_COLS)
    dma = lambda n: pltpu.SemaphoreType.DMA((n,))
    vmem = pl.BlockSpec(memory_space=pltpu.VMEM)
    analysis, mixing = pl.pallas_call(
        functools.partial(kernel, members, spaces),
        out_shape=(
            jax.ShapeDtypeStruct((fields, rows * lines, LANES), F32),
            jax.ShapeDtypeStruct((members, members), F32),
        ),
        in_specs=[vmem] * 7,
        out_specs=(vmem, vmem),
        scratch_shapes=[
            pltpu.VMEM((2, rows, fields, lines, LANES), F32),
            pltpu.VMEM((rows, lines, LANES), F32),
            pltpu.VMEM((2, fields, lines, LANES), F32),
            pltpu.VMEM((2, fields, lines, LANES), F32),
            pltpu.VMEM(block, F32),
            pltpu.VMEM(block, F32),
            pltpu.VMEM((samples, LANES), F32),
            pltpu.VMEM((PARTS * BEAM_ROWS, BEAM_COLS), F32),
            pltpu.VMEM((spaces,) + share, F32),
            pltpu.VMEM((spaces,) + share, F32),
            pltpu.VMEM((members * 2 * share[0], LANES), F32),
            pltpu.VMEM((members, LANES), F32),
            pltpu.VMEM((spaces, members, LANES), F32),
            pltpu.VMEM(block, F32),
            pltpu.VMEM(block, F32),
            dma(4 * fields), dma(4 * fields),
            dma(members), dma(members),
            dma(spaces), dma(spaces),
            dma(members), dma(members),
            dma(spaces), dma(spaces),
            dma(members), dma(members),
        ],
        compiler_params=pltpu.CompilerParams(
            collective_id=0, has_side_effects=True, vmem_limit_bytes=40 << 20
        ),
    )(
        mixed_rows.reshape(fields, lines * rows, LANES),
        visc_rows.reshape(lines * rows, LANES),
        cell_index.reshape(samples, LANES),
        beam_id.reshape(samples, LANES),
        los_weight.reshape(3, samples, LANES),
        observed.reshape(beams, LANES),
        obs_variance.reshape(beams, LANES),
    )
    analysis = analysis.reshape(fields, lines, rows, LANES).transpose(0, 2, 1, 3)
    return analysis.reshape(realization_fields.shape), mixing


def solution(mesh):
    return jax.shard_map(
        functools.partial(shards, mesh.shape["member"], mesh.shape["space"]),
        mesh=mesh,
        in_specs=(
            P("member", None, "space", None),
            P("space", None),
            P("space", None),
            P("space", None),
            P("space", None, None),
            P(),
            P(),
        ),
        out_specs=(P("member", None, "space", None), P()),
        check_vma=False,
    )
```

```python
import functools

import jax
import jax.numpy as jnp
from jax import lax
from jax.experimental import pallas as pl
from jax.experimental.pallas import tpu as pltpu
from jax.sharding import PartitionSpec as P

NS_STEPS = 8
COURANT = 0.5
BUOYANCY = 0.2
FIELDS = 4
LANES = 128
HALF = 64
BEAM_ROWS = 64
BEAM_COLS = 256
PARTS = 2
LINES = 128
BATCH = 16
BATCHES = LINES // BATCH
MESH = pl.DeviceIdType.MESH
F32 = jnp.float32
BF16 = jnp.bfloat16
HIGHEST = lax.Precision.HIGHEST


def bf16_iota(shape, dim):
    return lax.broadcasted_iota(jnp.int32, shape, dim).astype(F32).astype(BF16)


def stencil(center, behind, ahead, viscous):
    lane = lax.broadcasted_iota(jnp.int32, center.shape, 1)
    depth = lane & (HALF - 1)
    rows = center.shape[0]
    swapped = pltpu.roll(center, HALF, 1)
    lateral = swapped + jnp.where(
        lane < HALF, pltpu.roll(swapped, 1, 0), pltpu.roll(swapped, rows - 1, 0)
    )
    above = jnp.where(depth == HALF - 1, 0.0, pltpu.roll(center, LANES - 1, 1))
    below = jnp.where(depth == 0, 0.0, pltpu.roll(center, 1, 1))
    laplace = behind + ahead + lateral + (above + below) - 6.0 * center
    return center - COURANT * (center - behind) + viscous * laplace


def kernel(
    members, spaces,
    fields_hbm, visc_hbm, cell_hbm, beam_hbm, weight_hbm, observed_hbm, variance_hbm,
    out_ref, mixing_ref,
    fields_ref, visc_ref, cell_ref, beam_ref, weight_ref, observed_ref, variance_ref,
    own, low, high, forecast, pointwise, sight, pair_sight, columns, scatter,
    beam_send, beam_recv, share, gathered, stats_send, stats_recv, mixed, returned,
    load_sem, halo_send_sem, halo_recv_sem, sight_send_sem, sight_recv_sem,
    there_send_sem, there_recv_sem, beam_send_sem, beam_recv_sem,
    gather_send_sem, gather_recv_sem, stats_send_sem, stats_recv_sem, back_send_sem, back_recv_sem,
):
    me = lax.axis_index("member")
    here = lax.axis_index("space")
    core = lax.rem(me, 2)
    pair = me + 1 - 2 * core
    nxt = lax.rem(here + 1, spaces)
    prv = lax.rem(here + spaces - 1, spaces)

    loads = [
        pltpu.make_async_copy(fields_hbm, fields_ref, load_sem.at[0]),
        pltpu.make_async_copy(visc_hbm, visc_ref, load_sem.at[1]),
        pltpu.make_async_copy(beam_hbm, beam_ref, load_sem.at[2]),
        pltpu.make_async_copy(cell_hbm, cell_ref, load_sem.at[3]),
        pltpu.make_async_copy(weight_hbm, weight_ref, load_sem.at[4]),
        pltpu.make_async_copy(observed_hbm, observed_ref, load_sem.at[5]),
        pltpu.make_async_copy(variance_hbm, variance_ref, load_sem.at[6]),
    ]
    for load in loads:
        load.start()

    def others(count, mine, act):
        def one(d, carry):
            act(lax.rem(mine + d, count))
            return carry

        lax.fori_loop(1, count, one, 0)

    barrier = pltpu.get_barrier_semaphore()

    def greet(member, space):
        pl.semaphore_signal(barrier, inc=1, device_id=(member, space), device_id_type=MESH)

    others(spaces, here, lambda t: greet(me, t))
    others(spaces, here, lambda t: greet(pair, t))
    others(members, me, lambda p: greet(p, here))

    loads[0].wait()
    loads[1].wait()

    def spread(source, parity, plane):
        for first, start, count in ((0, LINES - 8, 8), (8, 0, LINES), (LINES + 8, 0, 8)):
            own[plane, pl.ds(first, count), :] = source[pl.ds(2 * start + parity, count, stride=2), :]

    for r in range(2):
        for f in range(FIELDS):
            spread(fields_ref.at[f], r, 1 + FIELDS * r + f)
        spread(visc_ref, r, 9 * r)
    pl.semaphore_wait(barrier, members + 2 * spaces - 3)

    def halo(n):
        lines = pl.ds(pl.multiple_of(BATCH * n, BATCH), BATCH)
        down = pltpu.make_async_remote_copy(
            src_ref=own.at[pl.ds(0, 9), lines], dst_ref=high.at[:, lines],
            send_sem=halo_send_sem.at[0, n], recv_sem=halo_recv_sem.at[0, n],
            device_id=(me, prv), device_id_type=MESH,
        )
        up = pltpu.make_async_remote_copy(
            src_ref=own.at[pl.ds(1, 9), lines], dst_ref=low.at[:, lines],
            send_sem=halo_send_sem.at[1, n], recv_sem=halo_recv_sem.at[1, n],
            device_id=(me, nxt), device_id_type=MESH,
        )
        return down, up

    def start_halo(n, carry):
        for copy in halo(n):
            copy.start()
        return carry

    lax.fori_loop(0, BATCHES, start_halo, 0)

    loads[2].wait()

    def fill_columns(k, carry):
        rows = pl.ds(pl.multiple_of(256 * core + 16 * k, 16), 16)
        beam_col = (beam_ref[rows, :] & (BEAM_COLS - 1)).astype(F32).astype(BF16)
        ids = bf16_iota((BEAM_COLS, LANES), 0)
        ones, zeros = jnp.ones((BEAM_COLS, LANES), BF16), jnp.zeros((BEAM_COLS, LANES), BF16)
        for g in range(16):
            columns[k, g * LANES : (g + 1) * LANES, :] = jnp.where(
                ids == beam_col[g : g + 1], ones, zeros
            ).T
        return carry

    lax.fori_loop(0, 2 * BATCHES, fill_columns, 0)
    for load in loads[3:]:
        load.wait()

    def step_batch(n):
        lines = pl.ds(pl.multiple_of(BATCH * n, BATCH), 2 * BATCH)
        viscous = [low[8, lines], own[0, lines], own[9, lines], high[0, lines]]
        for group in ((2, 3), (0,), (1,)):
            rows = {
                f: [low[f, lines], low[4 + f, lines], own[1 + f, lines],
                    own[5 + f, lines], high[1 + f, lines], high[5 + f, lines]]
                for f in group
            }
            for depth in (4, 2):
                nu = viscous if depth == 4 else viscous[1:3]
                after = {
                    f: [
                        stencil(rows[f][i + 1], rows[f][i], rows[f][i + 2], nu[i])
                        for i in range(depth)
                    ]
                    for f in group
                }
                if len(group) == 2:
                    lift, heat = group
                    after[lift] = [
                        after[lift][i] + BUOYANCY * rows[heat][i + 1] for i in range(depth)
                    ]
                    after[heat] = [
                        after[heat][i] - BUOYANCY * rows[lift][i + 1] for i in range(depth)
                    ]
                rows = after
            for f in group:
                for r in range(2):
                    for h in range(2):
                        block = members // 2 * r + 2 * n + h
                        forecast[block, f] = rows[f][r][8 + 8 * h : 16 + 8 * h]

    def gather_batch(n):
        for r in range(2):
            for h in range(2):
                block = members // 2 * r + 2 * n + h
                for g in range(2):
                    rows = pl.ds(pl.multiple_of(16 * block + 8 * g, 8), 8)
                    cells = cell_ref[rows, :]
                    lane, line = cells & (LANES - 1), cells >> 7
                    total = None
                    for c in range(3):
                        table = forecast[block, c]
                        value = None
                        for t in range(8):
                            row = jnp.broadcast_to(table[t : t + 1], (8, LANES))
                            found = jnp.take_along_axis(
                                row, lane, axis=1, mode="promise_in_bounds"
                            )
                            value = found if value is None else jnp.where(line == t, found, value)
                        term = weight_ref[c, rows, :] * value
                        total = term if total is None else total + term
                    sight[r, n, 16 * h + 8 * g : 16 * h + 8 * g + 8, :] = total

    def pair_copy(n):
        return pltpu.make_async_remote_copy(
            src_ref=sight.at[1 - core, n], dst_ref=pair_sight.at[n],
            send_sem=sight_send_sem.at[n], recv_sem=sight_recv_sem.at[n],
            device_id=(pair, here), device_id_type=MESH,
        )

    def scatter_batch(n):
        ids = bf16_iota((BEAM_ROWS, LANES), 0)
        zeros = jnp.zeros((BEAM_ROWS, LANES), BF16)
        product = None
        for h in range(2):
            parts = []
            for rest in (
                sight[core, n, 16 * h : 16 * h + 16, :], pair_sight[n, 16 * h : 16 * h + 16, :]
            ):
                for _ in range(PARTS):
                    part = rest.astype(BF16)
                    parts.append(part)
                    rest = rest - part.astype(F32)
            rows = pl.ds(pl.multiple_of(256 * core + 32 * n + 16 * h, 16), 16)
            beam_row = (beam_ref[rows, :] >> 8).astype(F32).astype(BF16)
            left = []
            for g in range(16):
                hit = ids == beam_row[g : g + 1]
                left.append(jnp.concatenate([
                    jnp.where(hit, jnp.broadcast_to(part[g : g + 1], (BEAM_ROWS, LANES)), zeros)
                    for part in parts
                ], axis=0))
            term = jnp.dot(
                jnp.concatenate(left, axis=1), columns[2 * n + h], preferred_element_type=F32
            )
            product = term if product is None else product + term
        scatter[...] += product

    def there(p):
        return pltpu.make_async_remote_copy(
            src_ref=forecast.at[p], dst_ref=pointwise.at[me],
            send_sem=there_send_sem.at[p], recv_sem=there_recv_sem.at[me],
            device_id=(p, here), device_id_type=MESH,
        )

    def there_from(i):
        return pltpu.make_async_remote_copy(
            src_ref=forecast.at[i], dst_ref=pointwise.at[i],
            send_sem=there_send_sem.at[i], recv_sem=there_recv_sem.at[i],
            device_id=(i, here), device_id_type=MESH,
        )

    scatter[...] = jnp.zeros_like(scatter)

    def finish_halo(n):
        for copy in halo(n):
            copy.wait_recv()

    finish_halo(0)
    for buffer in (low, high):
        buffer[:, LINES : LINES + BATCH, :] = buffer[:, 0:BATCH, :]
    finish_halo(1)
    step_batch(0)
    gather_batch(0)
    pair_copy(0).start()

    def batch(n, carry):
        @pl.when(n < BATCHES - 1)
        def _():
            finish_halo(n + 1)

        step_batch(n)
        pair_copy(n - 1).wait_recv()
        scatter_batch(n - 1)
        gather_batch(n)
        pair_copy(n).start()
        return carry

    lax.fori_loop(1, BATCHES, batch, 0)
    pair_copy(BATCHES - 1).wait_recv()
    scatter_batch(BATCHES - 1)
    for half in range(2):
        first = 2 * BEAM_ROWS * half
        total = scatter[first : first + BEAM_ROWS] + scatter[first + BEAM_ROWS : first + 2 * BEAM_ROWS]
        beam_send[half] = total.reshape(beam_send.shape[1:])

    def beam_to(half, t):
        return pltpu.make_async_remote_copy(
            src_ref=beam_send.at[half, t], dst_ref=beam_recv.at[half, here],
            send_sem=beam_send_sem.at[half, t], recv_sem=beam_recv_sem.at[half, here],
            device_id=(pair if half else me, t), device_id_type=MESH,
        )

    def beam_from(half, t):
        return pltpu.make_async_remote_copy(
            src_ref=beam_send.at[half, t], dst_ref=beam_recv.at[half, t],
            send_sem=beam_send_sem.at[half, t], recv_sem=beam_recv_sem.at[half, t],
            device_id=(pair if half else me, t), device_id_type=MESH,
        )

    others(spaces, here, lambda t: beam_to(0, t).start())
    others(spaces, here, lambda t: beam_to(1, t).start())
    beam_to(1, here).start()
    beam_recv[0, here] = beam_send[0, here]
    others(members, me, lambda p: there(p).start())
    pointwise[me] = forecast[me]
    beam_from(1, here).wait_recv()
    others(spaces, here, lambda t: beam_from(0, t).wait_recv())
    others(spaces, here, lambda t: beam_from(1, t).wait_recv())
    predicted = beam_recv[0, 0] + beam_recv[1, 0]
    for t in range(1, spaces):
        predicted = predicted + (beam_recv[0, t] + beam_recv[1, t])

    for half in range(2):
        share[half] = predicted[:, half * LANES : (half + 1) * LANES]

    def slot(i):
        return gathered.at[pl.ds(pl.multiple_of(8 * i, 8), 8), :]

    def share_to(p):
        return pltpu.make_async_remote_copy(
            src_ref=share.at[lax.rem(p, 2)], dst_ref=slot(me),
            send_sem=gather_send_sem.at[p], recv_sem=gather_recv_sem.at[me],
            device_id=(p, here), device_id_type=MESH,
        )

    def share_from(i):
        return pltpu.make_async_remote_copy(
            src_ref=share.at[core], dst_ref=slot(i),
            send_sem=gather_send_sem.at[i], recv_sem=gather_recv_sem.at[i],
            device_id=(i, here), device_id_type=MESH,
        )

    others(members, me, lambda p: share_to(p).start())
    gathered[pl.ds(pl.multiple_of(8 * me, 8), 8), :] = share[core]
    others(members, me, lambda i: share_from(i).wait_recv())

    every = jnp.concatenate(
        [gathered[pl.ds(sub, members, stride=8), :] for sub in range(8)], axis=1
    )
    mine = pl.ds(pl.multiple_of(16 * here, 16), 16)

    def core_rows(ref):
        rows = ref[mine, :]
        return jnp.concatenate([
            jnp.where(core == 0, rows[2 * i : 2 * i + 1], rows[2 * i + 1 : 2 * i + 2])
            for i in range(8)
        ], axis=1)

    seen, variance = core_rows(observed_ref), core_rows(variance_ref)
    mean_pred = jnp.mean(every, axis=0, keepdims=True)
    anomaly = every - mean_pred
    scaled = anomaly / variance
    member_id = lax.broadcasted_iota(jnp.int32, anomaly.shape, 0)
    against = jnp.where(member_id == members - 1, seen - mean_pred, anomaly)
    partial = lax.dot_general(
        scaled, against, (((1,), (1,)), ((), ())), precision=HIGHEST, preferred_element_type=F32
    )
    stats_send[...] = jnp.concatenate([partial[8 * g : 8 * g + 8] for g in range(members // 8)], axis=1)

    def stats_copy(other, t, origin_core, origin):
        return pltpu.make_async_remote_copy(
            src_ref=stats_send, dst_ref=stats_recv.at[origin_core, origin],
            send_sem=stats_send_sem.at[other, t], recv_sem=stats_recv_sem.at[origin_core, origin],
            device_id=(pair if other else me, t), device_id_type=MESH,
        )

    def stats_to(other, t):
        return stats_copy(other, t, core, here)

    def stats_from(other, t):
        return stats_copy(other, t, 1 - core if other else core, t)

    others(spaces, here, lambda t: stats_to(0, t).start())
    others(spaces, here, lambda t: stats_to(1, t).start())
    stats_to(1, here).start()
    stats_recv[core, here] = stats_send[...]
    stats_from(1, here).wait_recv()
    others(spaces, here, lambda t: stats_from(0, t).wait_recv())
    others(spaces, here, lambda t: stats_from(1, t).wait_recv())
    packed = stats_recv[0, 0] + stats_recv[1, 0]
    for t in range(1, spaces):
        packed = packed + (stats_recv[0, t] + stats_recv[1, t])
    stats = jnp.concatenate(
        [packed[:, members * g : members * (g + 1)] for g in range(members // 8)], axis=0
    )

    def times(a, b):
        return jnp.dot(a, b, precision=HIGHEST, preferred_element_type=F32)

    row_id = lax.broadcasted_iota(jnp.int32, (members, members), 0)
    col_id = lax.broadcasted_iota(jnp.int32, (members, members), 1)
    last = col_id == members - 1
    rest = jnp.sum(jnp.where(last, 0.0, stats), axis=1, keepdims=True)
    covar = jnp.where(last, -rest, stats)
    identity = jnp.where(row_id == col_id, 1.0, 0.0).astype(F32)
    system = identity + covar / (members - 1.0)
    magnitude = jnp.sqrt(jnp.sum(system * system, axis=(0, 1), keepdims=True))
    iterate = system / magnitude
    inverse_root = identity
    for _ in range(NS_STEPS):
        factor = 1.5 * identity - 0.5 * times(inverse_root, iterate)
        iterate = times(iterate, factor)
        inverse_root = times(factor, inverse_root)
    root_part = inverse_root / jnp.sqrt(magnitude)
    inverse_full = times(inverse_root, inverse_root) / magnitude
    shift = times(inverse_full, stats)[:, members - 1 : members] / (members - 1.0)
    combined = root_part + shift
    mixing = combined - jnp.mean(combined, axis=0, keepdims=True) + 1.0 / members
    mixing_ref[...] = mixing

    others(members, me, lambda i: there_from(i).wait_recv())
    count = FIELDS * 8
    block = jnp.concatenate(
        [pointwise.reshape(members * count, LANES)[pl.ds(k, members, stride=count), :] for k in range(count)],
        axis=1,
    )
    analysed = lax.dot_general(
        mixing, block, (((0,), (0,)), ((), ())), precision=HIGHEST, preferred_element_type=F32
    )
    for k in range(count):
        mixed.reshape(members * count, LANES)[pl.ds(k, members, stride=count), :] = (
            analysed[:, k * LANES : (k + 1) * LANES]
        )

    def back(j):
        return pltpu.make_async_remote_copy(
            src_ref=mixed.at[j], dst_ref=returned.at[me],
            send_sem=back_send_sem.at[j], recv_sem=back_recv_sem.at[me],
            device_id=(j, here), device_id_type=MESH,
        )

    def back_from(p):
        return pltpu.make_async_remote_copy(
            src_ref=mixed.at[p], dst_ref=returned.at[p],
            send_sem=back_send_sem.at[p], recv_sem=back_recv_sem.at[p],
            device_id=(p, here), device_id_type=MESH,
        )

    others(members, me, lambda j: back(j).start())
    returned[me] = mixed[me]

    def finish_send(n, carry):
        for copy in halo(n):
            copy.wait_send()
        pair_copy(n).wait_send()
        return carry

    lax.fori_loop(0, BATCHES, finish_send, 0)
    others(members, me, lambda p: there(p).wait_send())
    beam_to(1, here).wait_send()
    stats_to(1, here).wait_send()
    for half in range(2):
        others(spaces, here, lambda t: beam_to(half, t).wait_send())
        others(spaces, here, lambda t: stats_to(half, t).wait_send())
    others(members, me, lambda p: share_to(p).wait_send())
    others(members, me, lambda p: back_from(p).wait_recv())
    for p in range(members):
        r, q = divmod(p, members // 2)
        for f in range(FIELDS):
            out_ref[f, pl.ds(16 * q + r, 8, stride=2), :] = returned[p, f]
    others(members, me, lambda j: back(j).wait_send())


def shards(members, spaces, realization_fields, viscosity, cell_index, beam_id, los_weight, observed, obs_variance):
    _, fields, rows, plane = realization_fields.shape
    lines = plane // LANES
    samples = cell_index.shape[1] // LANES
    beams = observed.shape[0] // LANES
    mixed_rows = realization_fields.reshape(fields, rows, lines, LANES).transpose(0, 2, 1, 3)
    visc_rows = viscosity.reshape(rows, lines, LANES).transpose(1, 0, 2)
    block = (members, FIELDS, 8, LANES)
    share = (BEAM_ROWS // spaces, BEAM_COLS)
    dma = lambda *shape: pltpu.SemaphoreType.DMA(shape)
    vmem = pl.BlockSpec(memory_space=pltpu.VMEM)
    analysis, mixing = pl.pallas_call(
        functools.partial(kernel, members, spaces),
        out_shape=(
            jax.ShapeDtypeStruct((fields, rows * lines, LANES), F32),
            jax.ShapeDtypeStruct((members, members), F32),
        ),
        in_specs=[pl.BlockSpec(memory_space=pl.ANY)] * 7,
        out_specs=(vmem, vmem),
        scratch_shapes=[
            pltpu.VMEM((fields, rows * lines, LANES), F32),
            pltpu.VMEM((rows * lines, LANES), F32),
            pltpu.VMEM((samples, LANES), jnp.int32),
            pltpu.VMEM((samples, LANES), jnp.int32),
            pltpu.VMEM((3, samples, LANES), F32),
            pltpu.VMEM((beams, LANES), F32),
            pltpu.VMEM((beams, LANES), F32),
            pltpu.VMEM((10, LINES + BATCH, LANES), F32),
            pltpu.VMEM((9, LINES + BATCH, LANES), F32),
            pltpu.VMEM((9, LINES + BATCH, LANES), F32),
            pltpu.VMEM(block, F32),
            pltpu.VMEM(block, F32),
            pltpu.VMEM((2, BATCHES, 32, LANES), F32),
            pltpu.VMEM((BATCHES, 32, LANES), F32),
            pltpu.VMEM((2 * BATCHES, 16 * LANES, BEAM_COLS), BF16),
            pltpu.VMEM((2 * PARTS * BEAM_ROWS, BEAM_COLS), F32),
            pltpu.VMEM((2, spaces) + share, F32),
            pltpu.VMEM((2, spaces) + share, F32),
            pltpu.VMEM((2, share[0], LANES), F32),
            pltpu.VMEM((members * share[0], LANES), F32),
            pltpu.VMEM((8, LANES), F32),
            pltpu.VMEM((2, spaces, 8, LANES), F32),
            pltpu.VMEM(block, F32),
            pltpu.VMEM(block, F32),
            dma(7),
            dma(2, BATCHES), dma(2, BATCHES),
            dma(BATCHES), dma(BATCHES),
            dma(members), dma(members),
            dma(2, spaces), dma(2, spaces),
            dma(members), dma(members),
            dma(2, spaces), dma(2, spaces),
            dma(members), dma(members),
        ],
        compiler_params=pltpu.CompilerParams(
            collective_id=0, has_side_effects=True, vmem_limit_bytes=60 << 20
        ),
    )(
        mixed_rows.reshape(fields, lines * rows, LANES),
        visc_rows.reshape(lines * rows, LANES),
        cell_index.reshape(samples, LANES),
        beam_id.reshape(samples, LANES),
        los_weight.reshape(3, samples, LANES),
        observed.reshape(beams, LANES),
        obs_variance.reshape(beams, LANES),
    )
    analysis = analysis.reshape(fields, lines, rows, LANES).transpose(0, 2, 1, 3)
    return analysis.reshape(realization_fields.shape), mixing


def solution(mesh):
    return jax.shard_map(
        functools.partial(shards, mesh.shape["member"], mesh.shape["space"]),
        mesh=mesh,
        in_specs=(
            P("member", None, "space", None),
            P("space", None),
            P("space", None),
            P("space", None),
            P("space", None, None),
            P(),
            P(),
        ),
        out_specs=(P("member", None, "space", None), P()),
        check_vma=False,
    )
```

```python
import functools

import jax
import jax.numpy as jnp
from jax import lax
from jax.experimental import pallas as pl
from jax.experimental.pallas import tpu as pltpu
from jax.sharding import PartitionSpec as P

NS_STEPS = 8
COURANT = 0.5
BUOYANCY = 0.2
FIELDS = 4
LANES = 128
HALF = 64
BEAM_ROWS = 64
BEAM_COLS = 256
PARTS = 2
LINES = 128
BATCH = 16
BATCHES = LINES // BATCH
SIDE = 4
RELAYS = 4
MESH = pl.DeviceIdType.MESH
F32 = jnp.float32
BF16 = jnp.bfloat16
HIGHEST = lax.Precision.HIGHEST


def bf16_iota(shape, dim):
    return lax.broadcasted_iota(jnp.int32, shape, dim).astype(F32).astype(BF16)


def stencil(center, behind, ahead, viscous):
    lane = lax.broadcasted_iota(jnp.int32, center.shape, 1)
    depth = lane & (HALF - 1)
    rows = center.shape[0]
    swapped = pltpu.roll(center, HALF, 1)
    lateral = swapped + jnp.where(
        lane < HALF, pltpu.roll(swapped, 1, 0), pltpu.roll(swapped, rows - 1, 0)
    )
    above = jnp.where(depth == HALF - 1, 0.0, pltpu.roll(center, LANES - 1, 1))
    below = jnp.where(depth == 0, 0.0, pltpu.roll(center, 1, 1))
    laplace = behind + ahead + lateral + (above + below) - 6.0 * center
    return center - COURANT * (center - behind) + viscous * laplace


def kernel(
    members, spaces,
    fields_hbm, visc_hbm, cell_hbm, beam_hbm, weight_hbm, observed_hbm, variance_hbm,
    out_ref, mixing_ref,
    fields_ref, visc_ref, cell_ref, beam_ref, weight_ref, observed_ref, variance_ref,
    own, low, high, forecast, pointwise, sight, pair_sight, columns, scatter,
    beam_send, beam_recv, share, gathered, stats_send, stats_recv, mixed, returned,
    load_sem, relay_sem, halo_send_sem, halo_recv_sem, sight_send_sem, sight_recv_sem,
    there_send_sem, there_recv_sem, beam_send_sem, beam_recv_sem,
    gather_send_sem, gather_recv_sem, stats_send_sem, stats_recv_sem, back_send_sem, back_recv_sem,
):
    me = lax.axis_index("member")
    here = lax.axis_index("space")
    core = lax.rem(me, 2)
    pair = me + 1 - 2 * core
    nxt = lax.rem(here + 1, spaces)
    prv = lax.rem(here + spaces - 1, spaces)

    loads = [
        pltpu.make_async_copy(fields_hbm, fields_ref, load_sem.at[0]),
        pltpu.make_async_copy(visc_hbm, visc_ref, load_sem.at[1]),
        pltpu.make_async_copy(beam_hbm, beam_ref, load_sem.at[2]),
        pltpu.make_async_copy(cell_hbm, cell_ref, load_sem.at[3]),
        pltpu.make_async_copy(weight_hbm, weight_ref, load_sem.at[4]),
        pltpu.make_async_copy(observed_hbm, observed_ref, load_sem.at[5]),
        pltpu.make_async_copy(variance_hbm, variance_ref, load_sem.at[6]),
    ]

    def others(count, mine, act):
        def one(d, carry):
            act(lax.rem(mine + d, count))
            return carry

        lax.fori_loop(1, count, one, 0)

    barrier = pltpu.get_barrier_semaphore()

    chip = me // 2
    across, along = chip // SIDE, lax.rem(chip, SIDE)

    def device_at(x, y):
        return 2 * (SIDE * lax.rem(x, SIDE) + lax.rem(y, SIDE)) + core

    near = (
        (me, nxt), (me, prv), (pair, here),
        (device_at(across + 1, along), here), (device_at(across + SIDE - 1, along), here),
        (device_at(across, along + 1), here), (device_at(across, along + SIDE - 1), here),
    )

    def greet(semaphore):
        for device in near:
            pl.semaphore_signal(semaphore, inc=1, device_id=device, device_id_type=MESH)

    def hand_on(k):
        if k > 0:
            pl.semaphore_wait(relay_sem.at[k - 1], len(near))
        if k < RELAYS:
            greet(relay_sem.at[k])

    greet(barrier)
    for load in loads:
        load.start()

    loads[0].wait()
    loads[1].wait()

    def spread(source, parity, plane):
        for first, start, count in ((0, LINES - 8, 8), (8, 0, LINES), (LINES + 8, 0, 8)):
            own[plane, pl.ds(first, count), :] = source[pl.ds(2 * start + parity, count, stride=2), :]

    for r in range(2):
        for f in range(FIELDS):
            spread(fields_ref.at[f], r, 1 + FIELDS * r + f)
        spread(visc_ref, r, 9 * r)
    pl.semaphore_wait(barrier, len(near))

    def halo(n):
        lines = pl.ds(pl.multiple_of(BATCH * n, BATCH), BATCH)
        down = pltpu.make_async_remote_copy(
            src_ref=own.at[pl.ds(0, 9), lines], dst_ref=high.at[:, lines],
            send_sem=halo_send_sem.at[0, n], recv_sem=halo_recv_sem.at[0, n],
            device_id=(me, prv), device_id_type=MESH,
        )
        up = pltpu.make_async_remote_copy(
            src_ref=own.at[pl.ds(1, 9), lines], dst_ref=low.at[:, lines],
            send_sem=halo_send_sem.at[1, n], recv_sem=halo_recv_sem.at[1, n],
            device_id=(me, nxt), device_id_type=MESH,
        )
        return down, up

    def start_halo(n):
        for copy in halo(n):
            copy.start()

    start_halo(0)
    start_halo(1)
    hand_on(0)

    loads[2].wait()

    def fill_columns(k, carry):
        @pl.when(lax.rem(k, 4) == 0)
        def _():
            start_halo(2 + k // 4)

        rows = pl.ds(pl.multiple_of(256 * core + 16 * k, 16), 16)
        beam_col = (beam_ref[rows, :] & (BEAM_COLS - 1)).astype(F32).astype(BF16)
        ids = bf16_iota((BEAM_COLS, LANES), 0)
        ones, zeros = jnp.ones((BEAM_COLS, LANES), BF16), jnp.zeros((BEAM_COLS, LANES), BF16)
        for g in range(16):
            columns[k, g * LANES : (g + 1) * LANES, :] = jnp.where(
                ids == beam_col[g : g + 1], ones, zeros
            ).T
        return carry

    lax.fori_loop(0, 2 * BATCHES, fill_columns, 0)
    for load in loads[3:]:
        load.wait()

    def step_batch(n):
        lines = pl.ds(pl.multiple_of(BATCH * n, BATCH), 2 * BATCH)
        viscous = [low[8, lines], own[0, lines], own[9, lines], high[0, lines]]
        for group in ((2, 3), (0,), (1,)):
            rows = {
                f: [low[f, lines], low[4 + f, lines], own[1 + f, lines],
                    own[5 + f, lines], high[1 + f, lines], high[5 + f, lines]]
                for f in group
            }
            for depth in (4, 2):
                nu = viscous if depth == 4 else viscous[1:3]
                after = {
                    f: [
                        stencil(rows[f][i + 1], rows[f][i], rows[f][i + 2], nu[i])
                        for i in range(depth)
                    ]
                    for f in group
                }
                if len(group) == 2:
                    lift, heat = group
                    after[lift] = [
                        after[lift][i] + BUOYANCY * rows[heat][i + 1] for i in range(depth)
                    ]
                    after[heat] = [
                        after[heat][i] - BUOYANCY * rows[lift][i + 1] for i in range(depth)
                    ]
                rows = after
            for f in group:
                for r in range(2):
                    for h in range(2):
                        block = members // 2 * r + 2 * n + h
                        forecast[block, f] = rows[f][r][8 + 8 * h : 16 + 8 * h]

    def gather_batch(n):
        for r in range(2):
            for h in range(2):
                block = members // 2 * r + 2 * n + h
                for g in range(2):
                    rows = pl.ds(pl.multiple_of(16 * block + 8 * g, 8), 8)
                    cells = cell_ref[rows, :]
                    lane, line = cells & (LANES - 1), cells >> 7
                    total = None
                    for c in range(3):
                        table = forecast[block, c]
                        value = None
                        for t in range(8):
                            row = jnp.broadcast_to(table[t : t + 1], (8, LANES))
                            found = jnp.take_along_axis(
                                row, lane, axis=1, mode="promise_in_bounds"
                            )
                            value = found if value is None else jnp.where(line == t, found, value)
                        term = weight_ref[c, rows, :] * value
                        total = term if total is None else total + term
                    sight[r, n, 16 * h + 8 * g : 16 * h + 8 * g + 8, :] = total

    def pair_copy(n):
        return pltpu.make_async_remote_copy(
            src_ref=sight.at[1 - core, n], dst_ref=pair_sight.at[n],
            send_sem=sight_send_sem.at[n], recv_sem=sight_recv_sem.at[n],
            device_id=(pair, here), device_id_type=MESH,
        )

    def scatter_batch(n):
        ids = bf16_iota((BEAM_ROWS, LANES), 0)
        zeros = jnp.zeros((BEAM_ROWS, LANES), BF16)
        product = None
        for h in range(2):
            parts = []
            for rest in (
                sight[core, n, 16 * h : 16 * h + 16, :], pair_sight[n, 16 * h : 16 * h + 16, :]
            ):
                for _ in range(PARTS):
                    part = rest.astype(BF16)
                    parts.append(part)
                    rest = rest - part.astype(F32)
            rows = pl.ds(pl.multiple_of(256 * core + 32 * n + 16 * h, 16), 16)
            beam_row = (beam_ref[rows, :] >> 8).astype(F32).astype(BF16)
            left = []
            for g in range(16):
                hit = ids == beam_row[g : g + 1]
                left.append(jnp.concatenate([
                    jnp.where(hit, jnp.broadcast_to(part[g : g + 1], (BEAM_ROWS, LANES)), zeros)
                    for part in parts
                ], axis=0))
            term = jnp.dot(
                jnp.concatenate(left, axis=1), columns[2 * n + h], preferred_element_type=F32
            )
            product = term if product is None else product + term
        scatter[...] += product

    def there(p):
        return pltpu.make_async_remote_copy(
            src_ref=forecast.at[p], dst_ref=pointwise.at[me],
            send_sem=there_send_sem.at[p], recv_sem=there_recv_sem.at[me],
            device_id=(p, here), device_id_type=MESH,
        )

    def there_from(i):
        return pltpu.make_async_remote_copy(
            src_ref=forecast.at[i], dst_ref=pointwise.at[i],
            send_sem=there_send_sem.at[i], recv_sem=there_recv_sem.at[i],
            device_id=(i, here), device_id_type=MESH,
        )

    scatter[...] = jnp.zeros_like(scatter)

    def finish_halo(n):
        for copy in halo(n):
            copy.wait_recv()

    def send_blocks(n):
        for r in range(2):
            for h in range(2):
                block = members // 2 * r + 2 * n + h

                @pl.when(block != me)
                def _():
                    there(block).start()

    def scatter_next(n):
        pair_copy(n).wait_recv()
        scatter_batch(n)

    def send_blocks(n):
        for r in range(2):
            for h in range(2):
                block = members // 2 * r + 2 * n + h

                @pl.when(block != me)
                def _():
                    there(block).start()

    hand_on(1)
    finish_halo(0)
    for buffer in (low, high):
        buffer[:, LINES : LINES + BATCH, :] = buffer[:, 0:BATCH, :]
    for n in range(2):
        finish_halo(n + 1)
        start_halo(BATCHES - 2 + n)
        step_batch(n)
        gather_batch(n)
        pair_copy(n).start()
        hand_on(2 + n)

    def batch(n, carry):
        finish_halo(n + 1)
        step_batch(n)
        pair_copy(n - 2).wait_recv()
        scatter_batch(n - 2)
        gather_batch(n)
        pair_copy(n).start()

        @pl.when(n == 2)
        def _():
            hand_on(RELAYS)

        @pl.when(n < 4)
        def _():
            send_blocks(2 * n - 4)
            send_blocks(2 * n - 3)

        @pl.when(n >= 4)
        def _():
            send_blocks(n)

        return carry

    lax.fori_loop(2, BATCHES - 2, batch, 0)
    scatter_next(BATCHES - 4)
    finish_halo(BATCHES - 1)
    step_batch(BATCHES - 2)
    pair_copy(BATCHES - 3).wait_recv()
    scatter_batch(BATCHES - 3)
    gather_batch(BATCHES - 2)
    pair_copy(BATCHES - 2).start()
    step_batch(BATCHES - 1)
    gather_batch(BATCHES - 1)
    pair_copy(BATCHES - 1).start()
    send_blocks(BATCHES - 2)
    send_blocks(BATCHES - 1)
    scatter_next(BATCHES - 2)
    scatter_next(BATCHES - 1)
    for half in range(2):
        first = 2 * BEAM_ROWS * half
        total = scatter[first : first + BEAM_ROWS] + scatter[first + BEAM_ROWS : first + 2 * BEAM_ROWS]
        beam_send[half] = total.reshape(beam_send.shape[1:])

    def beam_to(half, t):
        return pltpu.make_async_remote_copy(
            src_ref=beam_send.at[half, t], dst_ref=beam_recv.at[half, here],
            send_sem=beam_send_sem.at[half, t], recv_sem=beam_recv_sem.at[half, here],
            device_id=(pair if half else me, t), device_id_type=MESH,
        )

    def beam_from(half, t):
        return pltpu.make_async_remote_copy(
            src_ref=beam_send.at[half, t], dst_ref=beam_recv.at[half, t],
            send_sem=beam_send_sem.at[half, t], recv_sem=beam_recv_sem.at[half, t],
            device_id=(pair if half else me, t), device_id_type=MESH,
        )

    others(spaces, here, lambda t: beam_to(0, t).start())
    others(spaces, here, lambda t: beam_to(1, t).start())
    beam_to(1, here).start()
    beam_recv[0, here] = beam_send[0, here]
    pointwise[me] = forecast[me]
    beam_from(1, here).wait_recv()
    others(spaces, here, lambda t: beam_from(0, t).wait_recv())
    others(spaces, here, lambda t: beam_from(1, t).wait_recv())
    predicted = beam_recv[0, 0] + beam_recv[1, 0]
    for t in range(1, spaces):
        predicted = predicted + (beam_recv[0, t] + beam_recv[1, t])

    for half in range(2):
        share[half] = predicted[:, half * LANES : (half + 1) * LANES]

    def slot(i):
        return gathered.at[pl.ds(pl.multiple_of(8 * i, 8), 8), :]

    def share_to(p):
        return pltpu.make_async_remote_copy(
            src_ref=share.at[lax.rem(p, 2)], dst_ref=slot(me),
            send_sem=gather_send_sem.at[p], recv_sem=gather_recv_sem.at[me],
            device_id=(p, here), device_id_type=MESH,
        )

    def share_from(i):
        return pltpu.make_async_remote_copy(
            src_ref=share.at[core], dst_ref=slot(i),
            send_sem=gather_send_sem.at[i], recv_sem=gather_recv_sem.at[i],
            device_id=(i, here), device_id_type=MESH,
        )

    others(members, me, lambda p: share_to(p).start())
    gathered[pl.ds(pl.multiple_of(8 * me, 8), 8), :] = share[core]
    others(members, me, lambda i: share_from(i).wait_recv())

    every = jnp.concatenate(
        [gathered[pl.ds(sub, members, stride=8), :] for sub in range(8)], axis=1
    )
    mine = pl.ds(pl.multiple_of(16 * here, 16), 16)

    def core_rows(ref):
        rows = ref[mine, :]
        return jnp.concatenate([
            jnp.where(core == 0, rows[2 * i : 2 * i + 1], rows[2 * i + 1 : 2 * i + 2])
            for i in range(8)
        ], axis=1)

    seen, variance = core_rows(observed_ref), core_rows(variance_ref)
    mean_pred = jnp.mean(every, axis=0, keepdims=True)
    anomaly = every - mean_pred
    scaled = anomaly / variance
    member_id = lax.broadcasted_iota(jnp.int32, anomaly.shape, 0)
    against = jnp.where(member_id == members - 1, seen - mean_pred, anomaly)
    partial = lax.dot_general(
        scaled, against, (((1,), (1,)), ((), ())), precision=HIGHEST, preferred_element_type=F32
    )
    stats_send[...] = jnp.concatenate([partial[8 * g : 8 * g + 8] for g in range(members // 8)], axis=1)

    def stats_copy(other, t, origin_core, origin):
        return pltpu.make_async_remote_copy(
            src_ref=stats_send, dst_ref=stats_recv.at[origin_core, origin],
            send_sem=stats_send_sem.at[other, t], recv_sem=stats_recv_sem.at[origin_core, origin],
            device_id=(pair if other else me, t), device_id_type=MESH,
        )

    def stats_to(other, t):
        return stats_copy(other, t, core, here)

    def stats_from(other, t):
        return stats_copy(other, t, 1 - core if other else core, t)

    others(spaces, here, lambda t: stats_to(0, t).start())
    others(spaces, here, lambda t: stats_to(1, t).start())
    stats_to(1, here).start()
    stats_recv[core, here] = stats_send[...]
    stats_from(1, here).wait_recv()
    others(spaces, here, lambda t: stats_from(0, t).wait_recv())
    others(spaces, here, lambda t: stats_from(1, t).wait_recv())
    packed = stats_recv[0, 0] + stats_recv[1, 0]
    for t in range(1, spaces):
        packed = packed + (stats_recv[0, t] + stats_recv[1, t])
    stats = jnp.concatenate(
        [packed[:, members * g : members * (g + 1)] for g in range(members // 8)], axis=0
    )

    def times(a, b):
        return jnp.dot(a, b, precision=HIGHEST, preferred_element_type=F32)

    row_id = lax.broadcasted_iota(jnp.int32, (members, members), 0)
    col_id = lax.broadcasted_iota(jnp.int32, (members, members), 1)
    last = col_id == members - 1
    rest = jnp.sum(jnp.where(last, 0.0, stats), axis=1, keepdims=True)
    covar = jnp.where(last, -rest, stats)
    identity = jnp.where(row_id == col_id, 1.0, 0.0).astype(F32)
    system = identity + covar / (members - 1.0)
    magnitude = jnp.sqrt(jnp.sum(system * system, axis=(0, 1), keepdims=True))
    iterate = system / magnitude
    inverse_root = identity
    for _ in range(NS_STEPS):
        factor = 1.5 * identity - 0.5 * times(inverse_root, iterate)
        iterate = times(iterate, factor)
        inverse_root = times(factor, inverse_root)
    root_part = inverse_root / jnp.sqrt(magnitude)
    inverse_full = times(inverse_root, inverse_root) / magnitude
    shift = times(inverse_full, stats)[:, members - 1 : members] / (members - 1.0)
    combined = root_part + shift
    mixing = combined - jnp.mean(combined, axis=0, keepdims=True) + 1.0 / members
    mixing_ref[...] = mixing

    others(members, me, lambda i: there_from(i).wait_recv())
    count = FIELDS * 8
    block = jnp.concatenate(
        [pointwise.reshape(members * count, LANES)[pl.ds(k, members, stride=count), :] for k in range(count)],
        axis=1,
    )
    analysed = lax.dot_general(
        mixing, block, (((0,), (0,)), ((), ())), precision=HIGHEST, preferred_element_type=F32
    )
    for k in range(count):
        mixed.reshape(members * count, LANES)[pl.ds(k, members, stride=count), :] = (
            analysed[:, k * LANES : (k + 1) * LANES]
        )

    def back(j):
        return pltpu.make_async_remote_copy(
            src_ref=mixed.at[j], dst_ref=returned.at[me],
            send_sem=back_send_sem.at[j], recv_sem=back_recv_sem.at[me],
            device_id=(j, here), device_id_type=MESH,
        )

    def back_from(p):
        return pltpu.make_async_remote_copy(
            src_ref=mixed.at[p], dst_ref=returned.at[p],
            send_sem=back_send_sem.at[p], recv_sem=back_recv_sem.at[p],
            device_id=(p, here), device_id_type=MESH,
        )

    others(members, me, lambda j: back(j).start())
    returned[me] = mixed[me]

    def finish_send(n, carry):
        for copy in halo(n):
            copy.wait_send()
        pair_copy(n).wait_send()
        return carry

    lax.fori_loop(0, BATCHES, finish_send, 0)
    others(members, me, lambda p: there(p).wait_send())
    beam_to(1, here).wait_send()
    stats_to(1, here).wait_send()
    for half in range(2):
        others(spaces, here, lambda t: beam_to(half, t).wait_send())
        others(spaces, here, lambda t: stats_to(half, t).wait_send())
    others(members, me, lambda p: share_to(p).wait_send())
    others(members, me, lambda p: back_from(p).wait_recv())
    for p in range(members):
        r, q = divmod(p, members // 2)
        for f in range(FIELDS):
            out_ref[f, pl.ds(16 * q + r, 8, stride=2), :] = returned[p, f]
    others(members, me, lambda j: back(j).wait_send())


def shards(members, spaces, realization_fields, viscosity, cell_index, beam_id, los_weight, observed, obs_variance):
    _, fields, rows, plane = realization_fields.shape
    lines = plane // LANES
    samples = cell_index.shape[1] // LANES
    beams = observed.shape[0] // LANES
    mixed_rows = realization_fields.reshape(fields, rows, lines, LANES).transpose(0, 2, 1, 3)
    visc_rows = viscosity.reshape(rows, lines, LANES).transpose(1, 0, 2)
    block = (members, FIELDS, 8, LANES)
    share = (BEAM_ROWS // spaces, BEAM_COLS)
    dma = lambda *shape: pltpu.SemaphoreType.DMA(shape)
    vmem = pl.BlockSpec(memory_space=pltpu.VMEM)
    analysis, mixing = pl.pallas_call(
        functools.partial(kernel, members, spaces),
        out_shape=(
            jax.ShapeDtypeStruct((fields, rows * lines, LANES), F32),
            jax.ShapeDtypeStruct((members, members), F32),
        ),
        in_specs=[pl.BlockSpec(memory_space=pl.ANY)] * 7,
        out_specs=(vmem, vmem),
        scratch_shapes=[
            pltpu.VMEM((fields, rows * lines, LANES), F32),
            pltpu.VMEM((rows * lines, LANES), F32),
            pltpu.VMEM((samples, LANES), jnp.int32),
            pltpu.VMEM((samples, LANES), jnp.int32),
            pltpu.VMEM((3, samples, LANES), F32),
            pltpu.VMEM((beams, LANES), F32),
            pltpu.VMEM((beams, LANES), F32),
            pltpu.VMEM((10, LINES + BATCH, LANES), F32),
            pltpu.VMEM((9, LINES + BATCH, LANES), F32),
            pltpu.VMEM((9, LINES + BATCH, LANES), F32),
            pltpu.VMEM(block, F32),
            pltpu.VMEM(block, F32),
            pltpu.VMEM((2, BATCHES, 32, LANES), F32),
            pltpu.VMEM((BATCHES, 32, LANES), F32),
            pltpu.VMEM((2 * BATCHES, 16 * LANES, BEAM_COLS), BF16),
            pltpu.VMEM((2 * PARTS * BEAM_ROWS, BEAM_COLS), F32),
            pltpu.VMEM((2, spaces) + share, F32),
            pltpu.VMEM((2, spaces) + share, F32),
            pltpu.VMEM((2, share[0], LANES), F32),
            pltpu.VMEM((members * share[0], LANES), F32),
            pltpu.VMEM((8, LANES), F32),
            pltpu.VMEM((2, spaces, 8, LANES), F32),
            pltpu.VMEM(block, F32),
            pltpu.VMEM(block, F32),
            dma(7), pltpu.SemaphoreType.REGULAR((RELAYS,)),
            dma(2, BATCHES), dma(2, BATCHES),
            dma(BATCHES), dma(BATCHES),
            dma(members), dma(members),
            dma(2, spaces), dma(2, spaces),
            dma(members), dma(members),
            dma(2, spaces), dma(2, spaces),
            dma(members), dma(members),
        ],
        compiler_params=pltpu.CompilerParams(
            collective_id=0, has_side_effects=True, vmem_limit_bytes=60 << 20
        ),
    )(
        mixed_rows.reshape(fields, lines * rows, LANES),
        visc_rows.reshape(lines * rows, LANES),
        cell_index.reshape(samples, LANES),
        beam_id.reshape(samples, LANES),
        los_weight.reshape(3, samples, LANES),
        observed.reshape(beams, LANES),
        obs_variance.reshape(beams, LANES),
    )
    analysis = analysis.reshape(fields, lines, rows, LANES).transpose(0, 2, 1, 3)
    return analysis.reshape(realization_fields.shape), mixing


def solution(mesh):
    return jax.shard_map(
        functools.partial(shards, mesh.shape["member"], mesh.shape["space"]),
        mesh=mesh,
        in_specs=(
            P("member", None, "space", None),
            P("space", None),
            P("space", None),
            P("space", None),
            P("space", None, None),
            P(),
            P(),
        ),
        out_specs=(P("member", None, "space", None), P()),
        check_vma=False,
    )
```

```python
import functools

import jax
import jax.numpy as jnp
from jax import lax
from jax.experimental import pallas as pl
from jax.experimental.pallas import tpu as pltpu
from jax.sharding import PartitionSpec as P

NS_STEPS = 8
COURANT = 0.5
BUOYANCY = 0.2
FIELDS = 4
LANES = 128
HALF = 64
BEAM_ROWS = 64
BEAM_COLS = 256
PARTS = 2
LINES = 128
BATCH = 16
BATCHES = LINES // BATCH
LAG = 2
SIDE = 4
RELAYS = 4
MESH = pl.DeviceIdType.MESH
F32 = jnp.float32
BF16 = jnp.bfloat16


def bf16_iota(shape, dim):
    return lax.broadcasted_iota(jnp.int32, shape, dim).astype(F32).astype(BF16)


def split(values, count):
    parts = []
    for _ in range(count):
        parts.append(values.astype(BF16))
        values = values - parts[-1].astype(F32)
    return parts


def times(a, b):
    a0, a1, a2 = split(a, 3)
    b0, b1, b2 = split(b, 3)
    n = a.shape[0]
    dot = functools.partial(jnp.dot, preferred_element_type=F32)
    first = dot(jnp.concatenate([a0, a1, a2], axis=0), b0)
    second = dot(jnp.concatenate([a0, a1], axis=0), b1)
    third = dot(a0, b2)
    small = second[n:] + (first[2 * n :] + third)
    return first[:n] + ((first[n : 2 * n] + second[:n]) + small)


def stencil(center, behind, ahead, viscous):
    lane = lax.broadcasted_iota(jnp.int32, center.shape, 1)
    depth = lane & (HALF - 1)
    rows = center.shape[0]
    swapped = pltpu.roll(center, HALF, 1)
    lateral = swapped + jnp.where(
        lane < HALF, pltpu.roll(swapped, 1, 0), pltpu.roll(swapped, rows - 1, 0)
    )
    above = jnp.where(depth == HALF - 1, 0.0, pltpu.roll(center, LANES - 1, 1))
    below = jnp.where(depth == 0, 0.0, pltpu.roll(center, 1, 1))
    laplace = behind + ahead + lateral + (above + below) - 6.0 * center
    return center - COURANT * (center - behind) + viscous * laplace


def kernel(
    members, spaces,
    fields_hbm, visc_hbm, cell_hbm, beam_hbm, weight_hbm, observed_hbm, variance_hbm,
    out_ref, mixing_ref,
    fields_ref, visc_ref, cell_ref, beam_ref, weight_ref, observed_ref, variance_ref,
    own, low, high, forecast, pointwise, sight, pair_sight, columns, scatter,
    beam_send, beam_recv, share, gathered, stats_send, stats_recv, mixed, returned,
    load_sem, relay_sem, halo_send_sem, halo_recv_sem, sight_send_sem, sight_recv_sem,
    there_send_sem, there_recv_sem, beam_send_sem, beam_recv_sem,
    gather_send_sem, gather_recv_sem, stats_send_sem, stats_recv_sem, back_send_sem, back_recv_sem,
):
    me = lax.axis_index("member")
    here = lax.axis_index("space")
    core = lax.rem(me, 2)
    pair = me + 1 - 2 * core
    nxt = lax.rem(here + 1, spaces)
    prv = lax.rem(here + spaces - 1, spaces)

    loads = [
        pltpu.make_async_copy(fields_hbm, fields_ref, load_sem.at[0]),
        pltpu.make_async_copy(visc_hbm, visc_ref, load_sem.at[1]),
        pltpu.make_async_copy(beam_hbm, beam_ref, load_sem.at[2]),
        pltpu.make_async_copy(cell_hbm, cell_ref, load_sem.at[3]),
        pltpu.make_async_copy(weight_hbm, weight_ref, load_sem.at[4]),
        pltpu.make_async_copy(observed_hbm, observed_ref, load_sem.at[5]),
        pltpu.make_async_copy(variance_hbm, variance_ref, load_sem.at[6]),
    ]

    chip = me // 2
    across, along = chip // SIDE, lax.rem(chip, SIDE)

    def device_at(x, y, side):
        return 2 * (SIDE * lax.rem(x, SIDE) + lax.rem(y, SIDE)) + side

    def ring(i):
        return lax.rem(6 - i + jnp.where(i >= 2, 7 - 2 * i, 0), SIDE)

    def other_members(act):
        def one(i, carry):
            flip = 1 - lax.rem(i, 2)
            side = core + flip - 2 * core * flip
            act(device_at(across + ring(i // 8), along + ring(lax.rem(i // 2, SIDE)), side))
            return carry

        lax.fori_loop(0, members - 1, one, 0)

    def other_spaces(act):
        def one(j, carry):
            step = (j + 1) // 2
            act(lax.rem(here + spaces // 2 + jnp.where(lax.rem(j, 2) == 1, spaces - step, step), spaces))
            return carry

        lax.fori_loop(0, spaces - 1, one, 0)

    barrier = pltpu.get_barrier_semaphore()

    near = (
        (me, nxt), (me, prv), (pair, here),
        (device_at(across + 1, along, core), here), (device_at(across + SIDE - 1, along, core), here),
        (device_at(across, along + 1, core), here), (device_at(across, along + SIDE - 1, core), here),
    )

    def greet(semaphore):
        for device in near:
            pl.semaphore_signal(semaphore, inc=1, device_id=device, device_id_type=MESH)

    def hand_on(k):
        if k > 0:
            pl.semaphore_wait(relay_sem.at[k - 1], len(near))
        if k < RELAYS:
            greet(relay_sem.at[k])

    greet(barrier)
    for load in loads:
        load.start()

    loads[0].wait()
    loads[1].wait()

    def spread(source, parity, plane):
        for first, start, count in ((0, LINES - 8, 8), (8, 0, LINES), (LINES + 8, 0, 8)):
            own[plane, pl.ds(first, count), :] = source[pl.ds(2 * start + parity, count, stride=2), :]

    def spread_field(f, carry):
        for r in range(2):
            spread(fields_ref.at[f], r, 1 + FIELDS * r + f)
        return carry

    lax.fori_loop(0, FIELDS, spread_field, 0)
    for r in range(2):
        spread(visc_ref, r, 9 * r)
    pl.semaphore_wait(barrier, len(near))

    def halo(n):
        lines = pl.ds(pl.multiple_of(BATCH * n, BATCH), BATCH)
        down = pltpu.make_async_remote_copy(
            src_ref=own.at[pl.ds(0, 9), lines], dst_ref=high.at[:, lines],
            send_sem=halo_send_sem.at[0, n], recv_sem=halo_recv_sem.at[0, n],
            device_id=(me, prv), device_id_type=MESH,
        )
        up = pltpu.make_async_remote_copy(
            src_ref=own.at[pl.ds(1, 9), lines], dst_ref=low.at[:, lines],
            send_sem=halo_send_sem.at[1, n], recv_sem=halo_recv_sem.at[1, n],
            device_id=(me, nxt), device_id_type=MESH,
        )
        return down, up

    def start_halo(n):
        for copy in halo(n):
            copy.start()

    start_halo(0)
    start_halo(1)
    hand_on(0)

    loads[2].wait()

    def fill_columns(k, carry):
        @pl.when(lax.rem(k, 8) == 0)
        def _():
            start_halo(2 + k // 8)

        rows = pl.ds(pl.multiple_of(256 * core + 8 * k, 8), 8)
        beam_col = (beam_ref[rows, :] & (BEAM_COLS - 1)).astype(F32).astype(BF16)
        ids = bf16_iota((BEAM_COLS, LANES), 0)
        ones, zeros = jnp.ones((BEAM_COLS, LANES), BF16), jnp.zeros((BEAM_COLS, LANES), BF16)
        for g in range(8):
            columns[k, g * LANES : (g + 1) * LANES, :] = jnp.where(
                ids == beam_col[g : g + 1], ones, zeros
            ).T
        return carry

    lax.fori_loop(0, 4 * BATCHES, fill_columns, 0)
    for load in loads[3:]:
        load.wait()

    def step_batch(n):
        lines = pl.ds(pl.multiple_of(BATCH * n, BATCH), 2 * BATCH)
        viscous = [low[8, lines], own[0, lines], own[9, lines], high[0, lines]]
        for group in ((2, 3), (0,), (1,)):
            rows = {
                f: [low[f, lines], low[4 + f, lines], own[1 + f, lines],
                    own[5 + f, lines], high[1 + f, lines], high[5 + f, lines]]
                for f in group
            }
            for depth in (4, 2):
                nu = viscous if depth == 4 else viscous[1:3]
                after = {
                    f: [
                        stencil(rows[f][i + 1], rows[f][i], rows[f][i + 2], nu[i])
                        for i in range(depth)
                    ]
                    for f in group
                }
                if len(group) == 2:
                    lift, heat = group
                    after[lift] = [
                        after[lift][i] + BUOYANCY * rows[heat][i + 1] for i in range(depth)
                    ]
                    after[heat] = [
                        after[heat][i] - BUOYANCY * rows[lift][i + 1] for i in range(depth)
                    ]
                rows = after
            for f in group:
                for r in range(2):
                    for h in range(2):
                        block = members // 2 * r + 2 * n + h
                        forecast[block, f] = rows[f][r][8 + 8 * h : 16 + 8 * h]

    def gather_batch(n):
        slot = lax.min(n, BATCHES)
        for r in range(2):
            for h in range(2):
                block = members // 2 * r + 2 * lax.min(n, BATCHES - 1) + h
                for g in range(2):
                    rows = pl.ds(pl.multiple_of(16 * block + 8 * g, 8), 8)
                    cells = cell_ref[rows, :]
                    lane, line = cells & (LANES - 1), cells >> 7
                    total = None
                    for c in range(3):
                        table = forecast[block, c]
                        value = None
                        for t in range(8):
                            row = jnp.broadcast_to(table[t : t + 1], (8, LANES))
                            found = jnp.take_along_axis(
                                row, lane, axis=1, mode="promise_in_bounds"
                            )
                            value = found if value is None else jnp.where(line == t, found, value)
                        term = weight_ref[c, rows, :] * value
                        total = term if total is None else total + term
                    sight[r, slot, 16 * h + 8 * g : 16 * h + 8 * g + 8, :] = total

    def pair_copy(n):
        return pltpu.make_async_remote_copy(
            src_ref=sight.at[1 - core, n], dst_ref=pair_sight.at[n],
            send_sem=sight_send_sem.at[n], recv_sem=sight_recv_sem.at[n],
            device_id=(pair, here), device_id_type=MESH,
        )

    def scatter_batch(n):
        ids = bf16_iota((BEAM_ROWS, LANES), 0)
        zeros = jnp.zeros((BEAM_ROWS, LANES), BF16)
        left = []
        for h in range(2):
            lines = slice(16 * h, 16 * h + 16)
            parts = split(sight[core, n, lines, :], PARTS) + split(pair_sight[n, lines, :], PARTS)
            rows = pl.ds(pl.multiple_of(256 * core + 32 * n + 16 * h, 16), 16)
            beam_row = (beam_ref[rows, :] >> 8).astype(F32).astype(BF16)
            for g in range(16):
                hit = ids == beam_row[g : g + 1]
                left.append(jnp.concatenate([
                    jnp.where(hit, jnp.broadcast_to(part[g : g + 1], (BEAM_ROWS, LANES)), zeros)
                    for part in parts
                ], axis=0))
        right = columns[pl.ds(4 * n, 4)].reshape(32 * LANES, BEAM_COLS)
        scatter[...] += jnp.dot(
            jnp.concatenate(left, axis=1), right, preferred_element_type=F32
        )

    def there(p):
        return pltpu.make_async_remote_copy(
            src_ref=forecast.at[p], dst_ref=pointwise.at[me],
            send_sem=there_send_sem.at[p], recv_sem=there_recv_sem.at[me],
            device_id=(p, here), device_id_type=MESH,
        )

    def there_from(i):
        return pltpu.make_async_remote_copy(
            src_ref=forecast.at[i], dst_ref=pointwise.at[i],
            send_sem=there_send_sem.at[i], recv_sem=there_recv_sem.at[i],
            device_id=(i, here), device_id_type=MESH,
        )

    scatter[...] = jnp.zeros_like(scatter)

    def finish_halo(n):
        for copy in halo(n):
            copy.wait_recv()

    def send_blocks(n):
        for r in range(2):
            for h in range(2):
                block = members // 2 * r + 2 * n + h

                @pl.when(block != me)
                def _():
                    there(block).start()

    hand_on(1)
    finish_halo(0)
    for buffer in (low, high):
        buffer[:, LINES : LINES + BATCH, :] = buffer[:, 0:BATCH, :]

    def first_batch(n, carry):
        finish_halo(n + 1)
        start_halo(BATCHES - LAG + n)
        step_batch(n)
        gather_batch(n)
        pair_copy(n).start()
        for k in range(LAG):
            @pl.when(n == k)
            def _():
                hand_on(2 + k)

        return carry

    def batch(n, carry):
        @pl.when(n < BATCHES - 1)
        def _():
            finish_halo(n + 1)

        @pl.when(n < BATCHES)
        def _():
            step_batch(n)

        pair_copy(n - LAG).wait_recv()
        scatter_batch(n - LAG)
        gather_batch(n)

        @pl.when(n < BATCHES)
        def _():
            pair_copy(n).start()

        @pl.when(n == LAG)
        def _():
            hand_on(RELAYS)

        def send_row(r, inner):
            def send_block(h, inner):
                block = members // 2 * r + 4 * (n - BATCHES // 2) + h

                @pl.when(block != me)
                def _():
                    there(block).start()

                return inner

            return lax.fori_loop(0, 4, send_block, inner)

        @pl.when(jnp.logical_and(n >= BATCHES // 2, n < BATCHES))
        def _():
            lax.fori_loop(0, 2, send_row, 0)

        return carry

    lax.fori_loop(0, LAG, first_batch, 0)
    lax.fori_loop(LAG, BATCHES + LAG, batch, 0)
    for half in range(2):
        first = 2 * BEAM_ROWS * half
        total = scatter[first : first + BEAM_ROWS] + scatter[first + BEAM_ROWS : first + 2 * BEAM_ROWS]
        beam_send[half] = total.reshape(beam_send.shape[1:])

    def beam_to(half, t):
        return pltpu.make_async_remote_copy(
            src_ref=beam_send.at[half, t], dst_ref=beam_recv.at[half, here],
            send_sem=beam_send_sem.at[half, t], recv_sem=beam_recv_sem.at[half, here],
            device_id=(pair if half else me, t), device_id_type=MESH,
        )

    def beam_from(half, t):
        return pltpu.make_async_remote_copy(
            src_ref=beam_send.at[half, t], dst_ref=beam_recv.at[half, t],
            send_sem=beam_send_sem.at[half, t], recv_sem=beam_recv_sem.at[half, t],
            device_id=(pair if half else me, t), device_id_type=MESH,
        )

    def send_share(t):
        beam_to(0, t).start()
        beam_to(1, t).start()

    other_spaces(send_share)
    beam_to(1, here).start()
    beam_recv[0, here] = beam_send[0, here]
    pointwise[me] = forecast[me]
    beam_from(1, here).wait_recv()
    other_spaces(lambda t: beam_from(0, t).wait_recv())
    other_spaces(lambda t: beam_from(1, t).wait_recv())
    predicted = beam_recv[0, 0] + beam_recv[1, 0]
    for t in range(1, spaces):
        predicted = predicted + (beam_recv[0, t] + beam_recv[1, t])

    for half in range(2):
        share[half] = predicted[:, half * LANES : (half + 1) * LANES]

    def slot(i):
        return gathered.at[pl.ds(pl.multiple_of(8 * i, 8), 8), :]

    def share_to(p):
        return pltpu.make_async_remote_copy(
            src_ref=share.at[lax.rem(p, 2)], dst_ref=slot(me),
            send_sem=gather_send_sem.at[p], recv_sem=gather_recv_sem.at[me],
            device_id=(p, here), device_id_type=MESH,
        )

    def share_from(i):
        return pltpu.make_async_remote_copy(
            src_ref=share.at[core], dst_ref=slot(i),
            send_sem=gather_send_sem.at[i], recv_sem=gather_recv_sem.at[i],
            device_id=(i, here), device_id_type=MESH,
        )

    other_members(lambda p: share_to(p).start())
    gathered[pl.ds(pl.multiple_of(8 * me, 8), 8), :] = share[core]
    other_members(lambda i: share_from(i).wait_recv())

    every = jnp.concatenate(
        [gathered[pl.ds(sub, members, stride=8), :] for sub in range(8)], axis=1
    )
    mine = pl.ds(pl.multiple_of(16 * here, 16), 16)

    def core_rows(ref):
        rows = ref[mine, :]
        return jnp.concatenate([
            jnp.where(core == 0, rows[2 * i : 2 * i + 1], rows[2 * i + 1 : 2 * i + 2])
            for i in range(8)
        ], axis=1)

    seen, variance = core_rows(observed_ref), core_rows(variance_ref)
    mean_pred = jnp.mean(every, axis=0, keepdims=True)
    anomaly = every - mean_pred
    scaled = anomaly / variance
    member_id = lax.broadcasted_iota(jnp.int32, anomaly.shape, 0)
    against = jnp.where(member_id == members - 1, seen - mean_pred, anomaly)
    product = lax.dot_general(
        jnp.concatenate(split(scaled, 3), axis=0), jnp.concatenate(split(against, 3), axis=0),
        (((1,), (1,)), ((), ())), preferred_element_type=F32,
    )

    def term(i, j):
        return product[members * i : members * (i + 1), members * j : members * (j + 1)]

    partial = term(0, 0) + ((term(0, 1) + term(1, 0)) + (term(1, 1) + (term(0, 2) + term(2, 0))))
    stats_send[...] = jnp.concatenate([partial[8 * g : 8 * g + 8] for g in range(members // 8)], axis=1)

    def stats_copy(other, t, origin_core, origin):
        return pltpu.make_async_remote_copy(
            src_ref=stats_send, dst_ref=stats_recv.at[origin_core, origin],
            send_sem=stats_send_sem.at[other, t], recv_sem=stats_recv_sem.at[origin_core, origin],
            device_id=(pair if other else me, t), device_id_type=MESH,
        )

    def stats_to(other, t):
        return stats_copy(other, t, core, here)

    def stats_from(other, t):
        return stats_copy(other, t, 1 - core if other else core, t)

    def send_stats(t):
        stats_to(0, t).start()
        stats_to(1, t).start()

    other_spaces(send_stats)
    stats_to(1, here).start()
    stats_recv[core, here] = stats_send[...]
    stats_from(1, here).wait_recv()
    other_spaces(lambda t: stats_from(0, t).wait_recv())
    other_spaces(lambda t: stats_from(1, t).wait_recv())
    packed = stats_recv[0, 0] + stats_recv[1, 0]
    for t in range(1, spaces):
        packed = packed + (stats_recv[0, t] + stats_recv[1, t])
    stats = jnp.concatenate(
        [packed[:, members * g : members * (g + 1)] for g in range(members // 8)], axis=0
    )

    row_id = lax.broadcasted_iota(jnp.int32, (members, members), 0)
    col_id = lax.broadcasted_iota(jnp.int32, (members, members), 1)
    last = col_id == members - 1
    rest = jnp.sum(jnp.where(last, 0.0, stats), axis=1, keepdims=True)
    covar = jnp.where(last, -rest, stats)
    identity = jnp.where(row_id == col_id, 1.0, 0.0).astype(F32)
    system = identity + covar / (members - 1.0)
    magnitude = jnp.sqrt(jnp.sum(system * system, axis=(0, 1), keepdims=True))
    iterate = system / magnitude

    def newton(_, pair_of):
        iterate, inverse_root = pair_of
        factor = 1.5 * identity - 0.5 * times(inverse_root, iterate)
        return times(iterate, factor), times(factor, inverse_root)

    _, inverse_root = lax.fori_loop(0, NS_STEPS, newton, (iterate, identity))
    root_part = inverse_root / jnp.sqrt(magnitude)
    inverse_full = times(inverse_root, inverse_root) / magnitude
    shift = times(inverse_full, stats)[:, members - 1 : members] / (members - 1.0)
    combined = root_part + shift
    mixing = combined - jnp.mean(combined, axis=0, keepdims=True) + 1.0 / members
    mixing_ref[...] = mixing

    other_members(lambda i: there_from(i).wait_recv())
    count = FIELDS * 8
    sources, targets = (ref.reshape(members * count, LANES) for ref in (pointwise, mixed))
    mix0, mix1 = split(mixing, 2)
    weights = jnp.concatenate([mix0, mix1, mix0, mix1], axis=0)

    def mix_field(f, carry):
        def lines(k):
            return pl.ds(8 * f + k, members, stride=count)

        block = jnp.concatenate([sources[lines(k), :] for k in range(8)], axis=1)
        block0, block1 = split(block, 2)
        analysed = lax.dot_general(
            weights, jnp.concatenate([block0, block0, block1, block1], axis=0),
            (((0,), (0,)), ((), ())), preferred_element_type=F32,
        )
        for k in range(8):
            targets[lines(k), :] = analysed[:, k * LANES : (k + 1) * LANES]
        return carry

    lax.fori_loop(0, FIELDS, mix_field, 0)

    def back(j):
        return pltpu.make_async_remote_copy(
            src_ref=mixed.at[j], dst_ref=returned.at[me],
            send_sem=back_send_sem.at[j], recv_sem=back_recv_sem.at[me],
            device_id=(j, here), device_id_type=MESH,
        )

    def back_from(p):
        return pltpu.make_async_remote_copy(
            src_ref=mixed.at[p], dst_ref=returned.at[p],
            send_sem=back_send_sem.at[p], recv_sem=back_recv_sem.at[p],
            device_id=(p, here), device_id_type=MESH,
        )

    other_members(lambda j: back(j).start())
    returned[me] = mixed[me]

    def finish_send(n, carry):
        for copy in halo(n):
            copy.wait_send()
        pair_copy(n).wait_send()
        return carry

    lax.fori_loop(0, BATCHES, finish_send, 0)
    other_members(lambda p: there(p).wait_send())
    beam_to(1, here).wait_send()
    stats_to(1, here).wait_send()
    for half in range(2):
        other_spaces(lambda t: beam_to(half, t).wait_send())
        other_spaces(lambda t: stats_to(half, t).wait_send())
    other_members(lambda p: share_to(p).wait_send())
    other_members(lambda p: back_from(p).wait_recv())
    for p in range(members):
        r, q = divmod(p, members // 2)
        for f in range(FIELDS):
            out_ref[f, pl.ds(16 * q + r, 8, stride=2), :] = returned[p, f]
    other_members(lambda j: back(j).wait_send())


def shards(members, spaces, realization_fields, viscosity, cell_index, beam_id, los_weight, observed, obs_variance):
    _, fields, rows, plane = realization_fields.shape
    lines = plane // LANES
    samples = cell_index.shape[1] // LANES
    beams = observed.shape[0] // LANES
    mixed_rows = realization_fields.reshape(fields, rows, lines, LANES).transpose(0, 2, 1, 3)
    visc_rows = viscosity.reshape(rows, lines, LANES).transpose(1, 0, 2)
    block = (members, FIELDS, 8, LANES)
    share = (BEAM_ROWS // spaces, BEAM_COLS)
    dma = lambda *shape: pltpu.SemaphoreType.DMA(shape)
    vmem = pl.BlockSpec(memory_space=pltpu.VMEM)
    analysis, mixing = pl.pallas_call(
        functools.partial(kernel, members, spaces),
        out_shape=(
            jax.ShapeDtypeStruct((fields, rows * lines, LANES), F32),
            jax.ShapeDtypeStruct((members, members), F32),
        ),
        in_specs=[pl.BlockSpec(memory_space=pl.ANY)] * 7,
        out_specs=(vmem, vmem),
        scratch_shapes=[
            pltpu.VMEM((fields, rows * lines, LANES), F32),
            pltpu.VMEM((rows * lines, LANES), F32),
            pltpu.VMEM((samples, LANES), jnp.int32),
            pltpu.VMEM((samples, LANES), jnp.int32),
            pltpu.VMEM((3, samples, LANES), F32),
            pltpu.VMEM((beams, LANES), F32),
            pltpu.VMEM((beams, LANES), F32),
            pltpu.VMEM((10, LINES + BATCH, LANES), F32),
            pltpu.VMEM((9, LINES + BATCH, LANES), F32),
            pltpu.VMEM((9, LINES + BATCH, LANES), F32),
            pltpu.VMEM(block, F32),
            pltpu.VMEM(block, F32),
            pltpu.VMEM((2, BATCHES + 1, 32, LANES), F32),
            pltpu.VMEM((BATCHES, 32, LANES), F32),
            pltpu.VMEM((4 * BATCHES, 8 * LANES, BEAM_COLS), BF16),
            pltpu.VMEM((2 * PARTS * BEAM_ROWS, BEAM_COLS), F32),
            pltpu.VMEM((2, spaces) + share, F32),
            pltpu.VMEM((2, spaces) + share, F32),
            pltpu.VMEM((2, share[0], LANES), F32),
            pltpu.VMEM((members * share[0], LANES), F32),
            pltpu.VMEM((8, LANES), F32),
            pltpu.VMEM((2, spaces, 8, LANES), F32),
            pltpu.VMEM(block, F32),
            pltpu.VMEM(block, F32),
            dma(7), pltpu.SemaphoreType.REGULAR((RELAYS,)),
            dma(2, BATCHES), dma(2, BATCHES),
            dma(BATCHES), dma(BATCHES),
            dma(members), dma(members),
            dma(2, spaces), dma(2, spaces),
            dma(members), dma(members),
            dma(2, spaces), dma(2, spaces),
            dma(members), dma(members),
        ],
        compiler_params=pltpu.CompilerParams(
            collective_id=0, has_side_effects=True, vmem_limit_bytes=60 << 20
        ),
    )(
        mixed_rows.reshape(fields, lines * rows, LANES),
        visc_rows.reshape(lines * rows, LANES),
        cell_index.reshape(samples, LANES),
        beam_id.reshape(samples, LANES),
        los_weight.reshape(3, samples, LANES),
        observed.reshape(beams, LANES),
        obs_variance.reshape(beams, LANES),
    )
    analysis = analysis.reshape(fields, lines, rows, LANES).transpose(0, 2, 1, 3)
    return analysis.reshape(realization_fields.shape), mixing


def solution(mesh):
    return jax.shard_map(
        functools.partial(shards, mesh.shape["member"], mesh.shape["space"]),
        mesh=mesh,
        in_specs=(
            P("member", None, "space", None),
            P("space", None),
            P("space", None),
            P("space", None),
            P("space", None, None),
            P(),
            P(),
        ),
        out_specs=(P("member", None, "space", None), P()),
        check_vma=False,
    )
```

```python
import functools

import jax
import jax.numpy as jnp
from jax import lax
from jax.experimental import pallas as pl
from jax.experimental.pallas import tpu as pltpu
from jax.sharding import PartitionSpec as P

NS_STEPS = 8
COURANT = 0.5
BUOYANCY = 0.2
FIELDS = 4
LANES = 128
HALF = 64
BEAM_ROWS = 64
BEAM_COLS = 256
PARTS = 2
LINES = 128
BATCH = 16
BATCHES = LINES // BATCH
LAG = 2
SIDE = 4
RELAYS = 4
MESH = pl.DeviceIdType.MESH
F32 = jnp.float32
BF16 = jnp.bfloat16


def bf16_iota(shape, dim):
    return lax.broadcasted_iota(jnp.int32, shape, dim).astype(F32).astype(BF16)


def split(values, count):
    parts = []
    for _ in range(count):
        parts.append(values.astype(BF16))
        values = values - parts[-1].astype(F32)
    return parts


def times(a, b):
    a0, a1, a2 = split(a, 3)
    b0, b1, b2 = split(b, 3)
    n = a.shape[0]
    dot = functools.partial(jnp.dot, preferred_element_type=F32)
    first = dot(jnp.concatenate([a0, a1, a2], axis=0), b0)
    second = dot(jnp.concatenate([a0, a1], axis=0), b1)
    third = dot(a0, b2)
    small = second[n:] + (first[2 * n :] + third)
    return first[:n] + ((first[n : 2 * n] + second[:n]) + small)


def stencil(center, behind, ahead, viscous):
    lane = lax.broadcasted_iota(jnp.int32, center.shape, 1)
    depth = lane & (HALF - 1)
    rows = center.shape[0]
    swapped = pltpu.roll(center, HALF, 1)
    lateral = swapped + jnp.where(
        lane < HALF, pltpu.roll(swapped, 1, 0), pltpu.roll(swapped, rows - 1, 0)
    )
    above = jnp.where(depth == HALF - 1, 0.0, pltpu.roll(center, LANES - 1, 1))
    below = jnp.where(depth == 0, 0.0, pltpu.roll(center, 1, 1))
    laplace = behind + ahead + lateral + (above + below) - 6.0 * center
    return center - COURANT * (center - behind) + viscous * laplace


def kernel(
    members, spaces,
    fields_hbm, visc_hbm, cell_hbm, beam_hbm, weight_hbm, observed_hbm, variance_hbm,
    out_ref, mixing_ref,
    fields_ref, visc_ref, cell_ref, beam_ref, weight_ref, observed_ref, variance_ref,
    own, low, high, forecast, pointwise, sight, pair_sight, columns, scatter,
    beam_send, beam_recv, share, gathered, stats_send, stats_recv, mixed, returned,
    load_sem, relay_sem, halo_send_sem, halo_recv_sem, sight_send_sem, sight_recv_sem,
    there_send_sem, there_recv_sem, beam_send_sem, beam_recv_sem,
    gather_send_sem, gather_recv_sem, stats_send_sem, stats_recv_sem, back_send_sem, back_recv_sem,
):
    me = lax.axis_index("member")
    here = lax.axis_index("space")
    core = lax.rem(me, 2)
    pair = me + 1 - 2 * core
    nxt = lax.rem(here + 1, spaces)
    prv = lax.rem(here + spaces - 1, spaces)

    loads = [
        pltpu.make_async_copy(fields_hbm, fields_ref, load_sem.at[0]),
        pltpu.make_async_copy(visc_hbm, visc_ref, load_sem.at[1]),
        pltpu.make_async_copy(beam_hbm, beam_ref, load_sem.at[2]),
        pltpu.make_async_copy(cell_hbm, cell_ref, load_sem.at[3]),
        pltpu.make_async_copy(weight_hbm, weight_ref, load_sem.at[4]),
        pltpu.make_async_copy(observed_hbm, observed_ref, load_sem.at[5]),
        pltpu.make_async_copy(variance_hbm, variance_ref, load_sem.at[6]),
    ]

    chip = me // 2
    across, along = chip // SIDE, lax.rem(chip, SIDE)

    def device_at(x, y, side):
        return 2 * (SIDE * lax.rem(x, SIDE) + lax.rem(y, SIDE)) + side

    def ring(i):
        return lax.rem(6 - i + jnp.where(i >= 2, 7 - 2 * i, 0), SIDE)

    def other_members(act, first=0, last=members - 1):
        def one(i, carry):
            flip = 1 - lax.rem(i, 2)
            side = core + flip - 2 * core * flip
            act(device_at(across + ring(i // 8), along + ring(lax.rem(i // 2, SIDE)), side))
            return carry

        lax.fori_loop(first, last, one, 0)

    def other_spaces(act):
        def one(j, carry):
            step = (j + 1) // 2
            act(lax.rem(here + spaces // 2 + jnp.where(lax.rem(j, 2) == 1, spaces - step, step), spaces))
            return carry

        lax.fori_loop(0, spaces - 1, one, 0)

    def finish(buffer, count, semaphore):
        part = buffer.at[pl.ds(0, count)]
        pltpu.make_async_copy(part, part, semaphore).wait()

    barrier = pltpu.get_barrier_semaphore()

    near = (
        (me, nxt), (me, prv), (pair, here),
        (device_at(across + 1, along, core), here), (device_at(across + SIDE - 1, along, core), here),
        (device_at(across, along + 1, core), here), (device_at(across, along + SIDE - 1, core), here),
    )

    def greet(semaphore):
        for device in near:
            pl.semaphore_signal(semaphore, inc=1, device_id=device, device_id_type=MESH)

    def hand_on(k):
        if k > 0:
            pl.semaphore_wait(relay_sem.at[k - 1], len(near))
        if k < RELAYS:
            greet(relay_sem.at[k])

    greet(barrier)
    for load in loads:
        load.start()

    loads[0].wait()
    loads[1].wait()

    def spread(source, parity, plane):
        for first, start, count in ((0, LINES - 8, 8), (8, 0, LINES), (LINES + 8, 0, 8)):
            own[plane, pl.ds(first, count), :] = source[pl.ds(2 * start + parity, count, stride=2), :]

    def spread_field(f, carry):
        for r in range(2):
            spread(fields_ref.at[f], r, 1 + FIELDS * r + f)
        return carry

    lax.fori_loop(0, FIELDS, spread_field, 0)
    for r in range(2):
        spread(visc_ref, r, 9 * r)
    pl.semaphore_wait(barrier, len(near))

    def halo(n):
        lines = pl.ds(pl.multiple_of(BATCH * n, BATCH), BATCH)
        down = pltpu.make_async_remote_copy(
            src_ref=own.at[pl.ds(0, 9), lines], dst_ref=high.at[:, lines],
            send_sem=halo_send_sem.at[0, n], recv_sem=halo_recv_sem.at[0, n],
            device_id=(me, prv), device_id_type=MESH,
        )
        up = pltpu.make_async_remote_copy(
            src_ref=own.at[pl.ds(1, 9), lines], dst_ref=low.at[:, lines],
            send_sem=halo_send_sem.at[1, n], recv_sem=halo_recv_sem.at[1, n],
            device_id=(me, nxt), device_id_type=MESH,
        )
        return down, up

    def start_halo(n):
        for copy in halo(n):
            copy.start()

    start_halo(0)
    start_halo(1)
    hand_on(0)

    loads[2].wait()

    def fill_columns(k, carry):
        @pl.when(lax.rem(k, 8) == 0)
        def _():
            start_halo(2 + k // 8)

        rows = pl.ds(pl.multiple_of(256 * core + 8 * k, 8), 8)
        beam_col = (beam_ref[rows, :] & (BEAM_COLS - 1)).astype(F32).astype(BF16)
        ids = bf16_iota((BEAM_COLS, LANES), 0)
        ones, zeros = jnp.ones((BEAM_COLS, LANES), BF16), jnp.zeros((BEAM_COLS, LANES), BF16)
        for g in range(8):
            columns[k, g * LANES : (g + 1) * LANES, :] = jnp.where(
                ids == beam_col[g : g + 1], ones, zeros
            ).T
        return carry

    lax.fori_loop(0, 4 * BATCHES, fill_columns, 0)
    for load in loads[3:]:
        load.wait()

    def step_batch(n):
        lines = pl.ds(pl.multiple_of(BATCH * n, BATCH), 2 * BATCH)
        viscous = [low[8, lines], own[0, lines], own[9, lines], high[0, lines]]
        for group in ((2, 3), (0,), (1,)):
            rows = {
                f: [low[f, lines], low[4 + f, lines], own[1 + f, lines],
                    own[5 + f, lines], high[1 + f, lines], high[5 + f, lines]]
                for f in group
            }
            for depth in (4, 2):
                nu = viscous if depth == 4 else viscous[1:3]
                after = {
                    f: [
                        stencil(rows[f][i + 1], rows[f][i], rows[f][i + 2], nu[i])
                        for i in range(depth)
                    ]
                    for f in group
                }
                if len(group) == 2:
                    lift, heat = group
                    after[lift] = [
                        after[lift][i] + BUOYANCY * rows[heat][i + 1] for i in range(depth)
                    ]
                    after[heat] = [
                        after[heat][i] - BUOYANCY * rows[lift][i + 1] for i in range(depth)
                    ]
                rows = after
            for f in group:
                for r in range(2):
                    for h in range(2):
                        block = members // 2 * r + 2 * n + h
                        forecast[block, f] = rows[f][r][8 + 8 * h : 16 + 8 * h]

    def gather_batch(n):
        slot = lax.min(n, BATCHES)
        for r in range(2):
            for h in range(2):
                block = members // 2 * r + 2 * lax.min(n, BATCHES - 1) + h
                for g in range(2):
                    rows = pl.ds(pl.multiple_of(16 * block + 8 * g, 8), 8)
                    cells = cell_ref[rows, :]
                    lane, line = cells & (LANES - 1), cells >> 7
                    total = None
                    for c in range(3):
                        table = forecast[block, c]
                        value = None
                        for t in range(8):
                            row = jnp.broadcast_to(table[t : t + 1], (8, LANES))
                            found = jnp.take_along_axis(
                                row, lane, axis=1, mode="promise_in_bounds"
                            )
                            value = found if value is None else jnp.where(line == t, found, value)
                        term = weight_ref[c, rows, :] * value
                        total = term if total is None else total + term
                    sight[r, slot, 16 * h + 8 * g : 16 * h + 8 * g + 8, :] = total

    def pair_copy(n):
        return pltpu.make_async_remote_copy(
            src_ref=sight.at[1 - core, n], dst_ref=pair_sight.at[n],
            send_sem=sight_send_sem.at[n], recv_sem=sight_recv_sem.at[n],
            device_id=(pair, here), device_id_type=MESH,
        )

    def scatter_batch(n):
        ids = bf16_iota((BEAM_ROWS, LANES), 0)
        zeros = jnp.zeros((BEAM_ROWS, LANES), BF16)
        left = []
        for h in range(2):
            lines = slice(16 * h, 16 * h + 16)
            parts = split(sight[core, n, lines, :], PARTS) + split(pair_sight[n, lines, :], PARTS)
            rows = pl.ds(pl.multiple_of(256 * core + 32 * n + 16 * h, 16), 16)
            beam_row = (beam_ref[rows, :] >> 8).astype(F32).astype(BF16)
            for g in range(16):
                hit = ids == beam_row[g : g + 1]
                left.append(jnp.concatenate([
                    jnp.where(hit, jnp.broadcast_to(part[g : g + 1], (BEAM_ROWS, LANES)), zeros)
                    for part in parts
                ], axis=0))
        right = columns[pl.ds(4 * n, 4)].reshape(32 * LANES, BEAM_COLS)
        scatter[...] += jnp.dot(
            jnp.concatenate(left, axis=1), right, preferred_element_type=F32
        )

    def there(p):
        return pltpu.make_async_remote_copy(
            src_ref=forecast.at[p], dst_ref=pointwise.at[me],
            send_sem=there_send_sem, recv_sem=there_recv_sem,
            device_id=(p, here), device_id_type=MESH,
        )

    scatter[...] = jnp.zeros_like(scatter)

    def finish_halo(n):
        for copy in halo(n):
            copy.wait_recv()

    def send_blocks(n):
        for r in range(2):
            for h in range(2):
                block = members // 2 * r + 2 * n + h

                @pl.when(block != me)
                def _():
                    there(block).start()

    hand_on(1)
    finish_halo(0)
    for buffer in (low, high):
        buffer[:, LINES : LINES + BATCH, :] = buffer[:, 0:BATCH, :]

    def first_batch(n, carry):
        finish_halo(n + 1)
        start_halo(BATCHES - LAG + n)
        step_batch(n)
        gather_batch(n)
        pair_copy(n).start()
        for k in range(LAG):
            @pl.when(n == k)
            def _():
                hand_on(2 + k)

        return carry

    def batch(n, carry):
        @pl.when(n < BATCHES - 1)
        def _():
            finish_halo(n + 1)

        @pl.when(n < BATCHES)
        def _():
            step_batch(n)

        pair_copy(n - LAG).wait_recv()
        scatter_batch(n - LAG)
        gather_batch(n)

        @pl.when(n < BATCHES)
        def _():
            pair_copy(n).start()

        @pl.when(n == LAG)
        def _():
            hand_on(RELAYS)

        return carry

    lax.fori_loop(0, LAG, first_batch, 0)
    lax.fori_loop(LAG, BATCHES + LAG, batch, 0)
    for half in range(2):
        first = 2 * BEAM_ROWS * half
        total = scatter[first : first + BEAM_ROWS] + scatter[first + BEAM_ROWS : first + 2 * BEAM_ROWS]
        beam_send[pl.ds(spaces * half, spaces)] = total.reshape((spaces,) + beam_send.shape[1:])

    def beam_to(half, t):
        return pltpu.make_async_remote_copy(
            src_ref=beam_send.at[spaces * half + t], dst_ref=beam_recv.at[spaces * half + here],
            send_sem=beam_send_sem, recv_sem=beam_recv_sem,
            device_id=(pair if half else me, t), device_id_type=MESH,
        )

    def send_share(t):
        beam_to(0, t).start()
        beam_to(1, t).start()

    other_spaces(send_share)
    beam_to(1, here).start()
    beam_recv[here] = beam_send[here]
    other_members(lambda p: there(p).start(), 0, members // 2)
    pointwise[me] = forecast[me]
    finish(beam_recv, 2 * spaces - 1, beam_recv_sem)
    predicted = beam_recv[0] + beam_recv[spaces]
    for t in range(1, spaces):
        predicted = predicted + (beam_recv[t] + beam_recv[spaces + t])

    for half in range(2):
        share[half] = predicted[:, half * LANES : (half + 1) * LANES]

    def slot(i):
        return gathered.at[pl.ds(pl.multiple_of(8 * i, 8), 8), :]

    def share_to(p):
        return pltpu.make_async_remote_copy(
            src_ref=share.at[lax.rem(p, 2)], dst_ref=slot(me),
            send_sem=gather_send_sem, recv_sem=gather_recv_sem,
            device_id=(p, here), device_id_type=MESH,
        )

    other_members(lambda p: share_to(p).start())
    gathered[pl.ds(pl.multiple_of(8 * me, 8), 8), :] = share[core]
    finish(gathered, 8 * (members - 1), gather_recv_sem)

    every = jnp.concatenate(
        [gathered[pl.ds(sub, members, stride=8), :] for sub in range(8)], axis=1
    )
    mine = pl.ds(pl.multiple_of(16 * here, 16), 16)

    def core_rows(ref):
        rows = ref[mine, :]
        return jnp.concatenate([
            jnp.where(core == 0, rows[2 * i : 2 * i + 1], rows[2 * i + 1 : 2 * i + 2])
            for i in range(8)
        ], axis=1)

    seen, variance = core_rows(observed_ref), core_rows(variance_ref)
    mean_pred = jnp.mean(every, axis=0, keepdims=True)
    anomaly = every - mean_pred
    scaled = anomaly / variance
    member_id = lax.broadcasted_iota(jnp.int32, anomaly.shape, 0)
    against = jnp.where(member_id == members - 1, seen - mean_pred, anomaly)
    product = lax.dot_general(
        jnp.concatenate(split(scaled, 3), axis=0), jnp.concatenate(split(against, 3), axis=0),
        (((1,), (1,)), ((), ())), preferred_element_type=F32,
    )

    def term(i, j):
        return product[members * i : members * (i + 1), members * j : members * (j + 1)]

    partial = term(0, 0) + ((term(0, 1) + term(1, 0)) + (term(1, 1) + (term(0, 2) + term(2, 0))))
    stats_send[...] = jnp.concatenate([partial[8 * g : 8 * g + 8] for g in range(members // 8)], axis=1)

    def stats_to(other, t):
        return pltpu.make_async_remote_copy(
            src_ref=stats_send, dst_ref=stats_recv.at[spaces * core + here],
            send_sem=stats_send_sem, recv_sem=stats_recv_sem,
            device_id=(pair if other else me, t), device_id_type=MESH,
        )

    def send_stats(t):
        stats_to(0, t).start()
        stats_to(1, t).start()

    other_spaces(send_stats)
    stats_to(1, here).start()
    other_members(lambda p: there(p).start(), members // 2)
    stats_recv[spaces * core + here] = stats_send[...]
    finish(stats_recv, 2 * spaces - 1, stats_recv_sem)
    packed = stats_recv[0] + stats_recv[spaces]
    for t in range(1, spaces):
        packed = packed + (stats_recv[t] + stats_recv[spaces + t])
    stats = jnp.concatenate(
        [packed[:, members * g : members * (g + 1)] for g in range(members // 8)], axis=0
    )

    row_id = lax.broadcasted_iota(jnp.int32, (members, members), 0)
    col_id = lax.broadcasted_iota(jnp.int32, (members, members), 1)
    last = col_id == members - 1
    rest = jnp.sum(jnp.where(last, 0.0, stats), axis=1, keepdims=True)
    covar = jnp.where(last, -rest, stats)
    identity = jnp.where(row_id == col_id, 1.0, 0.0).astype(F32)
    system = identity + covar / (members - 1.0)
    magnitude = jnp.sqrt(jnp.sum(system * system, axis=(0, 1), keepdims=True))
    iterate = system / magnitude

    def newton(_, pair_of):
        iterate, inverse_root = pair_of
        factor = 1.5 * identity - 0.5 * times(inverse_root, iterate)
        return times(iterate, factor), times(factor, inverse_root)

    _, inverse_root = lax.fori_loop(0, NS_STEPS, newton, (iterate, identity))
    root_part = inverse_root / jnp.sqrt(magnitude)
    inverse_full = times(inverse_root, inverse_root) / magnitude
    shift = times(inverse_full, stats)[:, members - 1 : members] / (members - 1.0)
    combined = root_part + shift
    mixing = combined - jnp.mean(combined, axis=0, keepdims=True) + 1.0 / members
    mixing_ref[...] = mixing

    finish(pointwise, members - 1, there_recv_sem)
    count = FIELDS * 8
    sources, targets = (ref.reshape(members * count, LANES) for ref in (pointwise, mixed))
    mix0, mix1 = split(mixing, 2)
    weights = jnp.concatenate([mix0, mix1, mix0, mix1], axis=0)

    def mix_field(f, carry):
        def lines(k):
            return pl.ds(8 * f + k, members, stride=count)

        block = jnp.concatenate([sources[lines(k), :] for k in range(8)], axis=1)
        block0, block1 = split(block, 2)
        analysed = lax.dot_general(
            weights, jnp.concatenate([block0, block0, block1, block1], axis=0),
            (((0,), (0,)), ((), ())), preferred_element_type=F32,
        )
        for k in range(8):
            targets[lines(k), :] = analysed[:, k * LANES : (k + 1) * LANES]
        return carry

    lax.fori_loop(0, FIELDS, mix_field, 0)

    def back(j):
        return pltpu.make_async_remote_copy(
            src_ref=mixed.at[j], dst_ref=returned.at[me],
            send_sem=back_send_sem, recv_sem=back_recv_sem,
            device_id=(j, here), device_id_type=MESH,
        )

    other_members(lambda j: back(j).start())
    returned[me] = mixed[me]

    def finish_send(n, carry):
        for copy in halo(n):
            copy.wait_send()
        pair_copy(n).wait_send()
        return carry

    lax.fori_loop(0, BATCHES, finish_send, 0)
    finish(forecast, members - 1, there_send_sem)
    finish(beam_send, 2 * spaces - 1, beam_send_sem)
    finish(stats_recv, 2 * spaces - 1, stats_send_sem)
    finish(gathered, 8 * (members - 1), gather_send_sem)
    finish(returned, members - 1, back_recv_sem)
    for p in range(members):
        r, q = divmod(p, members // 2)
        for f in range(FIELDS):
            out_ref[f, pl.ds(16 * q + r, 8, stride=2), :] = returned[p, f]
    finish(mixed, members - 1, back_send_sem)


def shards(members, spaces, realization_fields, viscosity, cell_index, beam_id, los_weight, observed, obs_variance):
    _, fields, rows, plane = realization_fields.shape
    lines = plane // LANES
    samples = cell_index.shape[1] // LANES
    beams = observed.shape[0] // LANES
    mixed_rows = realization_fields.reshape(fields, rows, lines, LANES).transpose(0, 2, 1, 3)
    visc_rows = viscosity.reshape(rows, lines, LANES).transpose(1, 0, 2)
    block = (members, FIELDS, 8, LANES)
    share = (BEAM_ROWS // spaces, BEAM_COLS)
    dma = lambda *shape: pltpu.SemaphoreType.DMA(shape)
    vmem = pl.BlockSpec(memory_space=pltpu.VMEM)
    analysis, mixing = pl.pallas_call(
        functools.partial(kernel, members, spaces),
        out_shape=(
            jax.ShapeDtypeStruct((fields, rows * lines, LANES), F32),
            jax.ShapeDtypeStruct((members, members), F32),
        ),
        in_specs=[pl.BlockSpec(memory_space=pl.ANY)] * 7,
        out_specs=(vmem, vmem),
        scratch_shapes=[
            pltpu.VMEM((fields, rows * lines, LANES), F32),
            pltpu.VMEM((rows * lines, LANES), F32),
            pltpu.VMEM((samples, LANES), jnp.int32),
            pltpu.VMEM((samples, LANES), jnp.int32),
            pltpu.VMEM((3, samples, LANES), F32),
            pltpu.VMEM((beams, LANES), F32),
            pltpu.VMEM((beams, LANES), F32),
            pltpu.VMEM((10, LINES + BATCH, LANES), F32),
            pltpu.VMEM((9, LINES + BATCH, LANES), F32),
            pltpu.VMEM((9, LINES + BATCH, LANES), F32),
            pltpu.VMEM(block, F32),
            pltpu.VMEM(block, F32),
            pltpu.VMEM((2, BATCHES + 1, 32, LANES), F32),
            pltpu.VMEM((BATCHES, 32, LANES), F32),
            pltpu.VMEM((4 * BATCHES, 8 * LANES, BEAM_COLS), BF16),
            pltpu.VMEM((2 * PARTS * BEAM_ROWS, BEAM_COLS), F32),
            pltpu.VMEM((2 * spaces,) + share, F32),
            pltpu.VMEM((2 * spaces,) + share, F32),
            pltpu.VMEM((2, share[0], LANES), F32),
            pltpu.VMEM((members * share[0], LANES), F32),
            pltpu.VMEM((8, LANES), F32),
            pltpu.VMEM((2 * spaces, 8, LANES), F32),
            pltpu.VMEM(block, F32),
            pltpu.VMEM(block, F32),
            dma(7), pltpu.SemaphoreType.REGULAR((RELAYS,)),
            dma(2, BATCHES), dma(2, BATCHES),
            dma(BATCHES), dma(BATCHES),
            *([pltpu.SemaphoreType.DMA] * 10),
        ],
        compiler_params=pltpu.CompilerParams(
            collective_id=0, has_side_effects=True, vmem_limit_bytes=60 << 20
        ),
    )(
        mixed_rows.reshape(fields, lines * rows, LANES),
        visc_rows.reshape(lines * rows, LANES),
        cell_index.reshape(samples, LANES),
        beam_id.reshape(samples, LANES),
        los_weight.reshape(3, samples, LANES),
        observed.reshape(beams, LANES),
        obs_variance.reshape(beams, LANES),
    )
    analysis = analysis.reshape(fields, lines, rows, LANES).transpose(0, 2, 1, 3)
    return analysis.reshape(realization_fields.shape), mixing


def solution(mesh):
    return jax.shard_map(
        functools.partial(shards, mesh.shape["member"], mesh.shape["space"]),
        mesh=mesh,
        in_specs=(
            P("member", None, "space", None),
            P("space", None),
            P("space", None),
            P("space", None),
            P("space", None, None),
            P(),
            P(),
        ),
        out_specs=(P("member", None, "space", None), P()),
        check_vma=False,
    )
```

```python
import functools

import jax
import jax.numpy as jnp
from jax import lax
from jax.experimental import pallas as pl
from jax.experimental.pallas import tpu as pltpu
from jax.sharding import PartitionSpec as P

NS_STEPS = 8
COURANT = 0.5
BUOYANCY = 0.2
FIELDS = 4
LANES = 128
HALF = 64
BEAM_ROWS = 64
BEAM_COLS = 256
PARTS = 2
LINES = 128
BATCH = 16
BATCHES = LINES // BATCH
LAG = 2
SIDE = 4
RELAYS = 4
MESH = pl.DeviceIdType.MESH
F32 = jnp.float32
BF16 = jnp.bfloat16


def bf16_iota(shape, dim):
    return lax.broadcasted_iota(jnp.int32, shape, dim).astype(F32).astype(BF16)


def split(values, count):
    parts = []
    for _ in range(count):
        parts.append(values.astype(BF16))
        values = values - parts[-1].astype(F32)
    return parts


def times(a, b):
    a0, a1, a2 = split(a, 3)
    b0, b1, b2 = split(b, 3)
    n = a.shape[0]
    dot = functools.partial(jnp.dot, preferred_element_type=F32)
    first = dot(jnp.concatenate([a0, a1, a2], axis=0), b0)
    second = dot(jnp.concatenate([a0, a1], axis=0), b1)
    third = dot(a0, b2)
    small = second[n:] + (first[2 * n :] + third)
    return first[:n] + ((first[n : 2 * n] + second[:n]) + small)


def stencil(center, behind, ahead, viscous):
    lane = lax.broadcasted_iota(jnp.int32, center.shape, 1)
    depth = lane & (HALF - 1)
    rows = center.shape[0]
    swapped = pltpu.roll(center, HALF, 1)
    lateral = swapped + jnp.where(
        lane < HALF, pltpu.roll(swapped, 1, 0), pltpu.roll(swapped, rows - 1, 0)
    )
    above = jnp.where(depth == HALF - 1, 0.0, pltpu.roll(center, LANES - 1, 1))
    below = jnp.where(depth == 0, 0.0, pltpu.roll(center, 1, 1))
    laplace = behind + ahead + lateral + (above + below) - 6.0 * center
    return center - COURANT * (center - behind) + viscous * laplace


def kernel(
    members, spaces,
    fields_hbm, visc_hbm, cell_hbm, beam_hbm, weight_hbm, observed_hbm, variance_hbm,
    out_ref, mixing_ref,
    fields_ref, visc_ref, cell_ref, beam_ref, weight_ref, observed_ref, variance_ref,
    own, low, high, forecast, pointwise, sight, pair_sight, columns, scatter,
    beam_send, beam_recv, share, gathered, stats_send, stats_recv, mixed, returned,
    load_sem, relay_sem, halo_send_sem, halo_recv_sem, sight_send_sem, sight_recv_sem,
    there_send_sem, there_recv_sem, beam_send_sem, beam_recv_sem,
    gather_send_sem, gather_recv_sem, stats_send_sem, stats_recv_sem, back_send_sem, back_recv_sem,
):
    me = lax.axis_index("member")
    here = lax.axis_index("space")
    core = lax.rem(me, 2)
    pair = me + 1 - 2 * core
    nxt = lax.rem(here + 1, spaces)
    prv = lax.rem(here + spaces - 1, spaces)

    loads = [
        pltpu.make_async_copy(fields_hbm, fields_ref, load_sem.at[0]),
        pltpu.make_async_copy(visc_hbm, visc_ref, load_sem.at[1]),
        pltpu.make_async_copy(beam_hbm, beam_ref, load_sem.at[2]),
        pltpu.make_async_copy(cell_hbm, cell_ref, load_sem.at[3]),
        pltpu.make_async_copy(weight_hbm, weight_ref, load_sem.at[4]),
        pltpu.make_async_copy(observed_hbm, observed_ref, load_sem.at[5]),
        pltpu.make_async_copy(variance_hbm, variance_ref, load_sem.at[6]),
    ]

    chip = me // 2
    across, along = chip // SIDE, lax.rem(chip, SIDE)

    def device_at(x, y, side):
        return 2 * (SIDE * lax.rem(x, SIDE) + lax.rem(y, SIDE)) + side

    steps_x = [lax.rem(across + i, SIDE) * (2 * SIDE) for i in range(SIDE)]
    steps_y = [lax.rem(along + i, SIDE) * 2 for i in range(SIDE)]
    sides = [core, 1 - core]
    far_first = sorted(
        ((x, y, side) for x in range(SIDE) for y in range(SIDE) for side in range(2)),
        key=lambda step: -min(step[0], SIDE - step[0]) - min(step[1], SIDE - step[1]),
    )
    far_first.remove((0, 0, 0))

    def other_members(act, first=0, last=members - 1):
        for x, y, side in far_first[first:last]:
            act(steps_x[x] + steps_y[y] + sides[side])

    def other_spaces(act):
        for step in sorted(range(1, spaces), key=lambda step: -min(step, spaces - step)):
            act(lax.rem(here + step, spaces))

    def finish(buffer, count, semaphore):
        part = buffer.at[pl.ds(0, count)]
        pltpu.make_async_copy(part, part, semaphore).wait()

    barrier = pltpu.get_barrier_semaphore()

    near = (
        (me, nxt), (me, prv), (pair, here),
        (device_at(across + 1, along, core), here), (device_at(across + SIDE - 1, along, core), here),
        (device_at(across, along + 1, core), here), (device_at(across, along + SIDE - 1, core), here),
    )

    def greet(semaphore):
        for device in near:
            pl.semaphore_signal(semaphore, inc=1, device_id=device, device_id_type=MESH)

    def hand_on(k):
        if k > 0:
            pl.semaphore_wait(relay_sem.at[k - 1], len(near))
        if k < RELAYS:
            greet(relay_sem.at[k])

    greet(barrier)
    for load in loads:
        load.start()

    loads[0].wait()
    loads[1].wait()

    def spread(source, parity, plane):
        for first, start, count in ((0, LINES - 8, 8), (8, 0, LINES), (LINES + 8, 0, 8)):
            own[plane, pl.ds(first, count), :] = source[pl.ds(2 * start + parity, count, stride=2), :]

    def spread_field(f, carry):
        for r in range(2):
            spread(fields_ref.at[f], r, 1 + FIELDS * r + f)
        return carry

    lax.fori_loop(0, FIELDS, spread_field, 0)
    for r in range(2):
        spread(visc_ref, r, 9 * r)
    pl.semaphore_wait(barrier, len(near))

    def halo(n):
        lines = pl.ds(pl.multiple_of(BATCH * n, BATCH), BATCH)
        down = pltpu.make_async_remote_copy(
            src_ref=own.at[pl.ds(0, 9), lines], dst_ref=high.at[:, lines],
            send_sem=halo_send_sem.at[0, n], recv_sem=halo_recv_sem.at[0, n],
            device_id=(me, prv), device_id_type=MESH,
        )
        up = pltpu.make_async_remote_copy(
            src_ref=own.at[pl.ds(1, 9), lines], dst_ref=low.at[:, lines],
            send_sem=halo_send_sem.at[1, n], recv_sem=halo_recv_sem.at[1, n],
            device_id=(me, nxt), device_id_type=MESH,
        )
        return down, up

    def start_halo(n):
        for copy in halo(n):
            copy.start()

    start_halo(0)
    start_halo(1)
    hand_on(0)

    loads[2].wait()

    def fill_columns(k, carry):
        @pl.when(lax.rem(k, 8) == 0)
        def _():
            start_halo(2 + k // 8)

        rows = pl.ds(pl.multiple_of(256 * core + 8 * k, 8), 8)
        beam_col = (beam_ref[rows, :] & (BEAM_COLS - 1)).astype(F32).astype(BF16)
        ids = bf16_iota((BEAM_COLS, LANES), 0)
        ones, zeros = jnp.ones((BEAM_COLS, LANES), BF16), jnp.zeros((BEAM_COLS, LANES), BF16)
        for g in range(8):
            columns[k, g * LANES : (g + 1) * LANES, :] = jnp.where(
                ids == beam_col[g : g + 1], ones, zeros
            ).T
        return carry

    lax.fori_loop(0, 4 * BATCHES, fill_columns, 0)
    for load in loads[3:]:
        load.wait()

    def step_batch(n):
        lines = pl.ds(pl.multiple_of(BATCH * n, BATCH), 2 * BATCH)
        viscous = [low[8, lines], own[0, lines], own[9, lines], high[0, lines]]
        for group in ((2, 3), (0,), (1,)):
            rows = {
                f: [low[f, lines], low[4 + f, lines], own[1 + f, lines],
                    own[5 + f, lines], high[1 + f, lines], high[5 + f, lines]]
                for f in group
            }
            for depth in (4, 2):
                nu = viscous if depth == 4 else viscous[1:3]
                after = {
                    f: [
                        stencil(rows[f][i + 1], rows[f][i], rows[f][i + 2], nu[i])
                        for i in range(depth)
                    ]
                    for f in group
                }
                if len(group) == 2:
                    lift, heat = group
                    after[lift] = [
                        after[lift][i] + BUOYANCY * rows[heat][i + 1] for i in range(depth)
                    ]
                    after[heat] = [
                        after[heat][i] - BUOYANCY * rows[lift][i + 1] for i in range(depth)
                    ]
                rows = after
            for f in group:
                for r in range(2):
                    for h in range(2):
                        block = members // 2 * r + 2 * n + h
                        forecast[block, f] = rows[f][r][8 + 8 * h : 16 + 8 * h]

    def gather_batch(n):
        slot = lax.min(n, BATCHES)
        for r in range(2):
            for h in range(2):
                block = members // 2 * r + 2 * lax.min(n, BATCHES - 1) + h
                for g in range(2):
                    rows = pl.ds(pl.multiple_of(16 * block + 8 * g, 8), 8)
                    cells = cell_ref[rows, :]
                    lane, line = cells & (LANES - 1), cells >> 7
                    total = None
                    for c in range(3):
                        table = forecast[block, c]
                        value = None
                        for t in range(8):
                            row = jnp.broadcast_to(table[t : t + 1], (8, LANES))
                            found = jnp.take_along_axis(
                                row, lane, axis=1, mode="promise_in_bounds"
                            )
                            value = found if value is None else jnp.where(line == t, found, value)
                        term = weight_ref[c, rows, :] * value
                        total = term if total is None else total + term
                    sight[r, slot, 16 * h + 8 * g : 16 * h + 8 * g + 8, :] = total

    def pair_copy(n):
        return pltpu.make_async_remote_copy(
            src_ref=sight.at[1 - core, n], dst_ref=pair_sight.at[n],
            send_sem=sight_send_sem.at[n], recv_sem=sight_recv_sem.at[n],
            device_id=(pair, here), device_id_type=MESH,
        )

    def scatter_batch(n):
        ids = bf16_iota((BEAM_ROWS, LANES), 0)
        zeros = jnp.zeros((BEAM_ROWS, LANES), BF16)
        left = []
        for h in range(2):
            lines = slice(16 * h, 16 * h + 16)
            parts = split(sight[core, n, lines, :], PARTS) + split(pair_sight[n, lines, :], PARTS)
            rows = pl.ds(pl.multiple_of(256 * core + 32 * n + 16 * h, 16), 16)
            beam_row = (beam_ref[rows, :] >> 8).astype(F32).astype(BF16)
            for g in range(16):
                hit = ids == beam_row[g : g + 1]
                left.append(jnp.concatenate([
                    jnp.where(hit, jnp.broadcast_to(part[g : g + 1], (BEAM_ROWS, LANES)), zeros)
                    for part in parts
                ], axis=0))
        right = columns[pl.ds(4 * n, 4)].reshape(32 * LANES, BEAM_COLS)
        scatter[...] += jnp.dot(
            jnp.concatenate(left, axis=1), right, preferred_element_type=F32
        )

    def there(p):
        return pltpu.make_async_remote_copy(
            src_ref=forecast.at[p], dst_ref=pointwise.at[me],
            send_sem=there_send_sem, recv_sem=there_recv_sem,
            device_id=(p, here), device_id_type=MESH,
        )

    scatter[...] = jnp.zeros_like(scatter)

    def finish_halo(n):
        for copy in halo(n):
            copy.wait_recv()

    def send_blocks(n):
        for r in range(2):
            for h in range(2):
                block = members // 2 * r + 2 * n + h

                @pl.when(block != me)
                def _():
                    there(block).start()

    hand_on(1)
    finish_halo(0)
    for buffer in (low, high):
        buffer[:, LINES : LINES + BATCH, :] = buffer[:, 0:BATCH, :]

    def first_batch(n, carry):
        finish_halo(n + 1)
        start_halo(BATCHES - LAG + n)
        step_batch(n)
        gather_batch(n)
        pair_copy(n).start()
        for k in range(LAG):
            @pl.when(n == k)
            def _():
                hand_on(2 + k)

        return carry

    def batch(n, carry):
        @pl.when(n < BATCHES - 1)
        def _():
            finish_halo(n + 1)

        @pl.when(n < BATCHES)
        def _():
            step_batch(n)

        pair_copy(n - LAG).wait_recv()
        scatter_batch(n - LAG)
        gather_batch(n)

        @pl.when(n < BATCHES)
        def _():
            pair_copy(n).start()

        @pl.when(n == LAG)
        def _():
            hand_on(RELAYS)

        return carry

    lax.fori_loop(0, LAG, first_batch, 0)
    lax.fori_loop(LAG, BATCHES + LAG, batch, 0)
    for half in range(2):
        first = 2 * BEAM_ROWS * half
        total = scatter[first : first + BEAM_ROWS] + scatter[first + BEAM_ROWS : first + 2 * BEAM_ROWS]
        beam_send[pl.ds(spaces * half, spaces)] = total.reshape((spaces,) + beam_send.shape[1:])

    def beam_to(half, t):
        return pltpu.make_async_remote_copy(
            src_ref=beam_send.at[spaces * half + t], dst_ref=beam_recv.at[spaces * half + here],
            send_sem=beam_send_sem, recv_sem=beam_recv_sem,
            device_id=(pair if half else me, t), device_id_type=MESH,
        )

    def send_share(t):
        beam_to(0, t).start()
        beam_to(1, t).start()

    other_spaces(send_share)
    beam_to(1, here).start()
    beam_recv[here] = beam_send[here]
    other_members(lambda p: there(p).start(), 0, members // 2)
    pointwise[me] = forecast[me]
    finish(beam_recv, 2 * spaces - 1, beam_recv_sem)
    predicted = beam_recv[0] + beam_recv[spaces]
    for t in range(1, spaces):
        predicted = predicted + (beam_recv[t] + beam_recv[spaces + t])

    for half in range(2):
        share[half] = predicted[:, half * LANES : (half + 1) * LANES]

    def slot(i):
        return gathered.at[pl.ds(pl.multiple_of(8 * i, 8), 8), :]

    def share_to(p):
        return pltpu.make_async_remote_copy(
            src_ref=share.at[lax.rem(p, 2)], dst_ref=slot(me),
            send_sem=gather_send_sem, recv_sem=gather_recv_sem,
            device_id=(p, here), device_id_type=MESH,
        )

    other_members(lambda p: share_to(p).start())
    gathered[pl.ds(pl.multiple_of(8 * me, 8), 8), :] = share[core]
    finish(gathered, 8 * (members - 1), gather_recv_sem)

    every = jnp.concatenate(
        [gathered[pl.ds(sub, members, stride=8), :] for sub in range(8)], axis=1
    )
    mine = pl.ds(pl.multiple_of(16 * here, 16), 16)

    def core_rows(ref):
        rows = ref[mine, :]
        return jnp.concatenate([
            jnp.where(core == 0, rows[2 * i : 2 * i + 1], rows[2 * i + 1 : 2 * i + 2])
            for i in range(8)
        ], axis=1)

    seen, variance = core_rows(observed_ref), core_rows(variance_ref)
    mean_pred = jnp.mean(every, axis=0, keepdims=True)
    anomaly = every - mean_pred
    scaled = anomaly / variance
    member_id = lax.broadcasted_iota(jnp.int32, anomaly.shape, 0)
    against = jnp.where(member_id == members - 1, seen - mean_pred, anomaly)
    product = lax.dot_general(
        jnp.concatenate(split(scaled, 3), axis=0), jnp.concatenate(split(against, 3), axis=0),
        (((1,), (1,)), ((), ())), preferred_element_type=F32,
    )

    def term(i, j):
        return product[members * i : members * (i + 1), members * j : members * (j + 1)]

    partial = term(0, 0) + ((term(0, 1) + term(1, 0)) + (term(1, 1) + (term(0, 2) + term(2, 0))))
    stats_send[...] = jnp.concatenate([partial[8 * g : 8 * g + 8] for g in range(members // 8)], axis=1)

    def stats_to(other, t):
        return pltpu.make_async_remote_copy(
            src_ref=stats_send, dst_ref=stats_recv.at[spaces * core + here],
            send_sem=stats_send_sem, recv_sem=stats_recv_sem,
            device_id=(pair if other else me, t), device_id_type=MESH,
        )

    def send_stats(t):
        stats_to(0, t).start()
        stats_to(1, t).start()

    other_spaces(send_stats)
    stats_to(1, here).start()
    other_members(lambda p: there(p).start(), members // 2)
    stats_recv[spaces * core + here] = stats_send[...]
    finish(stats_recv, 2 * spaces - 1, stats_recv_sem)
    packed = stats_recv[0] + stats_recv[spaces]
    for t in range(1, spaces):
        packed = packed + (stats_recv[t] + stats_recv[spaces + t])
    stats = jnp.concatenate(
        [packed[:, members * g : members * (g + 1)] for g in range(members // 8)], axis=0
    )

    row_id = lax.broadcasted_iota(jnp.int32, (members, members), 0)
    col_id = lax.broadcasted_iota(jnp.int32, (members, members), 1)
    last = col_id == members - 1
    rest = jnp.sum(jnp.where(last, 0.0, stats), axis=1, keepdims=True)
    covar = jnp.where(last, -rest, stats)
    identity = jnp.where(row_id == col_id, 1.0, 0.0).astype(F32)
    system = identity + covar / (members - 1.0)
    magnitude = jnp.sqrt(jnp.sum(system * system, axis=(0, 1), keepdims=True))
    iterate = system / magnitude

    def newton(_, pair_of):
        iterate, inverse_root = pair_of
        factor = 1.5 * identity - 0.5 * times(inverse_root, iterate)
        return times(iterate, factor), times(factor, inverse_root)

    factor = 1.5 * identity - 0.5 * iterate
    _, inverse_root = lax.fori_loop(1, NS_STEPS, newton, (times(iterate, factor), factor))
    root_part = inverse_root / jnp.sqrt(magnitude)
    inverse_full = times(inverse_root, inverse_root) / magnitude
    shift = times(inverse_full, stats)[:, members - 1 : members] / (members - 1.0)
    combined = root_part + shift
    mixing = combined - jnp.mean(combined, axis=0, keepdims=True) + 1.0 / members
    mixing_ref[...] = mixing

    finish(pointwise, members - 1, there_recv_sem)
    count = FIELDS * 8
    sources, targets = (ref.reshape(members * count, LANES) for ref in (pointwise, mixed))
    mix0, mix1 = split(mixing, 2)
    weights = jnp.concatenate([mix0, mix1, mix0, mix1], axis=0)

    def mix_field(f, carry):
        def lines(k):
            return pl.ds(8 * f + k, members, stride=count)

        block = jnp.concatenate([sources[lines(k), :] for k in range(8)], axis=1)
        block0, block1 = split(block, 2)
        analysed = lax.dot_general(
            weights, jnp.concatenate([block0, block0, block1, block1], axis=0),
            (((0,), (0,)), ((), ())), preferred_element_type=F32,
        )
        for k in range(8):
            targets[lines(k), :] = analysed[:, k * LANES : (k + 1) * LANES]
        return carry

    lax.fori_loop(0, FIELDS, mix_field, 0)

    def back(j):
        return pltpu.make_async_remote_copy(
            src_ref=mixed.at[j], dst_ref=returned.at[me],
            send_sem=back_send_sem, recv_sem=back_recv_sem,
            device_id=(j, here), device_id_type=MESH,
        )

    other_members(lambda j: back(j).start())
    returned[me] = mixed[me]

    def finish_send(n, carry):
        for copy in halo(n):
            copy.wait_send()
        pair_copy(n).wait_send()
        return carry

    lax.fori_loop(0, BATCHES, finish_send, 0)
    finish(forecast, members - 1, there_send_sem)
    finish(beam_send, 2 * spaces - 1, beam_send_sem)
    finish(stats_recv, 2 * spaces - 1, stats_send_sem)
    finish(gathered, 8 * (members - 1), gather_send_sem)
    finish(returned, members - 1, back_recv_sem)
    for p in range(members):
        r, q = divmod(p, members // 2)
        for f in range(FIELDS):
            out_ref[f, pl.ds(16 * q + r, 8, stride=2), :] = returned[p, f]
    finish(mixed, members - 1, back_send_sem)


def shards(members, spaces, realization_fields, viscosity, cell_index, beam_id, los_weight, observed, obs_variance):
    _, fields, rows, plane = realization_fields.shape
    lines = plane // LANES
    samples = cell_index.shape[1] // LANES
    beams = observed.shape[0] // LANES
    mixed_rows = realization_fields.reshape(fields, rows, lines, LANES).transpose(0, 2, 1, 3)
    visc_rows = viscosity.reshape(rows, lines, LANES).transpose(1, 0, 2)
    block = (members, FIELDS, 8, LANES)
    share = (BEAM_ROWS // spaces, BEAM_COLS)
    dma = lambda *shape: pltpu.SemaphoreType.DMA(shape)
    vmem = pl.BlockSpec(memory_space=pltpu.VMEM)
    analysis, mixing = pl.pallas_call(
        functools.partial(kernel, members, spaces),
        out_shape=(
            jax.ShapeDtypeStruct((fields, rows * lines, LANES), F32),
            jax.ShapeDtypeStruct((members, members), F32),
        ),
        in_specs=[pl.BlockSpec(memory_space=pl.ANY)] * 7,
        out_specs=(vmem, vmem),
        scratch_shapes=[
            pltpu.VMEM((fields, rows * lines, LANES), F32),
            pltpu.VMEM((rows * lines, LANES), F32),
            pltpu.VMEM((samples, LANES), jnp.int32),
            pltpu.VMEM((samples, LANES), jnp.int32),
            pltpu.VMEM((3, samples, LANES), F32),
            pltpu.VMEM((beams, LANES), F32),
            pltpu.VMEM((beams, LANES), F32),
            pltpu.VMEM((10, LINES + BATCH, LANES), F32),
            pltpu.VMEM((9, LINES + BATCH, LANES), F32),
            pltpu.VMEM((9, LINES + BATCH, LANES), F32),
            pltpu.VMEM(block, F32),
            pltpu.VMEM(block, F32),
            pltpu.VMEM((2, BATCHES + 1, 32, LANES), F32),
            pltpu.VMEM((BATCHES, 32, LANES), F32),
            pltpu.VMEM((4 * BATCHES, 8 * LANES, BEAM_COLS), BF16),
            pltpu.VMEM((2 * PARTS * BEAM_ROWS, BEAM_COLS), F32),
            pltpu.VMEM((2 * spaces,) + share, F32),
            pltpu.VMEM((2 * spaces,) + share, F32),
            pltpu.VMEM((2, share[0], LANES), F32),
            pltpu.VMEM((members * share[0], LANES), F32),
            pltpu.VMEM((8, LANES), F32),
            pltpu.VMEM((2 * spaces, 8, LANES), F32),
            pltpu.VMEM(block, F32),
            pltpu.VMEM(block, F32),
            dma(7), pltpu.SemaphoreType.REGULAR((RELAYS,)),
            dma(2, BATCHES), dma(2, BATCHES),
            dma(BATCHES), dma(BATCHES),
            *([pltpu.SemaphoreType.DMA] * 10),
        ],
        compiler_params=pltpu.CompilerParams(
            collective_id=0, has_side_effects=True, vmem_limit_bytes=60 << 20
        ),
    )(
        mixed_rows.reshape(fields, lines * rows, LANES),
        visc_rows.reshape(lines * rows, LANES),
        cell_index.reshape(samples, LANES),
        beam_id.reshape(samples, LANES),
        los_weight.reshape(3, samples, LANES),
        observed.reshape(beams, LANES),
        obs_variance.reshape(beams, LANES),
    )
    analysis = analysis.reshape(fields, lines, rows, LANES).transpose(0, 2, 1, 3)
    return analysis.reshape(realization_fields.shape), mixing


def solution(mesh):
    return jax.shard_map(
        functools.partial(shards, mesh.shape["member"], mesh.shape["space"]),
        mesh=mesh,
        in_specs=(
            P("member", None, "space", None),
            P("space", None),
            P("space", None),
            P("space", None),
            P("space", None, None),
            P(),
            P(),
        ),
        out_specs=(P("member", None, "space", None), P()),
        check_vma=False,
    )
```

```python
import functools

import jax
import jax.numpy as jnp
from jax import lax
from jax.experimental import pallas as pl
from jax.experimental.pallas import tpu as pltpu
from jax.sharding import PartitionSpec as P

NS_STEPS = 8
COURANT = 0.5
BUOYANCY = 0.2
FIELDS = 4
LANES = 128
HALF = 64
BEAM_ROWS = 64
BEAM_COLS = 256
PARTS = 2
LINES = 128
BATCH = 16
BATCHES = LINES // BATCH
LAG = 2
SIDE = 4
RELAYS = 4
MESH = pl.DeviceIdType.MESH
F32 = jnp.float32
BF16 = jnp.bfloat16


def bf16_iota(shape, dim):
    return lax.broadcasted_iota(jnp.int32, shape, dim).astype(F32).astype(BF16)


def split(values, count):
    parts = []
    for _ in range(count):
        parts.append(values.astype(BF16))
        values = values - parts[-1].astype(F32)
    return parts


def times(a, b):
    a0, a1, a2 = split(a, 3)
    b0, b1, b2 = split(b, 3)
    n = a.shape[0]
    dot = functools.partial(jnp.dot, preferred_element_type=F32)
    first = dot(jnp.concatenate([a0, a1, a2], axis=0), b0)
    second = dot(jnp.concatenate([a0, a1], axis=0), b1)
    third = dot(a0, b2)
    small = second[n:] + (first[2 * n :] + third)
    return first[:n] + ((first[n : 2 * n] + second[:n]) + small)


def stencil(center, behind, ahead, viscous):
    lane = lax.broadcasted_iota(jnp.int32, center.shape, 1)
    depth = lane & (HALF - 1)
    rows = center.shape[0]
    swapped = pltpu.roll(center, HALF, 1)
    lateral = swapped + jnp.where(
        lane < HALF, pltpu.roll(swapped, 1, 0), pltpu.roll(swapped, rows - 1, 0)
    )
    above = jnp.where(depth == HALF - 1, 0.0, pltpu.roll(center, LANES - 1, 1))
    below = jnp.where(depth == 0, 0.0, pltpu.roll(center, 1, 1))
    laplace = behind + ahead + lateral + (above + below) - 6.0 * center
    return center - COURANT * (center - behind) + viscous * laplace


def kernel(
    members, spaces,
    fields_hbm, visc_hbm, cell_hbm, beam_hbm, weight_hbm, observed_hbm, variance_hbm,
    out_hbm, mixing_ref,
    out_ref, fields_ref, visc_ref, cell_ref, beam_ref, weight_ref, observed_ref, variance_ref,
    own, low, high, forecast, pointwise, sight, pair_sight, columns, scatter,
    beam_send, beam_recv, share, gathered, stats_send, stats_recv, mixed, returned,
    load_sem, store_sem, relay_sem, halo_send_sem, halo_recv_sem, sight_send_sem, sight_recv_sem,
    there_send_sem, there_recv_sem, beam_send_sem, beam_recv_sem,
    gather_send_sem, gather_recv_sem, stats_send_sem, stats_recv_sem, back_send_sem, back_recv_sem,
):
    me = lax.axis_index("member")
    here = lax.axis_index("space")
    core = lax.rem(me, 2)
    pair = me + 1 - 2 * core
    nxt = lax.rem(here + 1, spaces)
    prv = lax.rem(here + spaces - 1, spaces)

    loads = [
        pltpu.make_async_copy(fields_hbm, fields_ref, load_sem.at[0]),
        pltpu.make_async_copy(visc_hbm, visc_ref, load_sem.at[1]),
        pltpu.make_async_copy(beam_hbm, beam_ref, load_sem.at[2]),
        pltpu.make_async_copy(cell_hbm, cell_ref, load_sem.at[3]),
        pltpu.make_async_copy(weight_hbm, weight_ref, load_sem.at[4]),
        pltpu.make_async_copy(observed_hbm, observed_ref, load_sem.at[5]),
        pltpu.make_async_copy(variance_hbm, variance_ref, load_sem.at[6]),
    ]

    chip = me // 2
    across, along = chip // SIDE, lax.rem(chip, SIDE)

    def device_at(x, y, side):
        return 2 * (SIDE * lax.rem(x, SIDE) + lax.rem(y, SIDE)) + side

    steps_x = [lax.rem(across + i, SIDE) * (2 * SIDE) for i in range(SIDE)]
    steps_y = [lax.rem(along + i, SIDE) * 2 for i in range(SIDE)]
    sides = [core, 1 - core]
    far_first = sorted(
        ((x, y, side) for x in range(SIDE) for y in range(SIDE) for side in range(2)),
        key=lambda step: -min(step[0], SIDE - step[0]) - min(step[1], SIDE - step[1]),
    )
    far_first.remove((0, 0, 0))

    def other_members(act, first=0, last=members - 1):
        for x, y, side in far_first[first:last]:
            act(steps_x[x] + steps_y[y] + sides[side])

    def other_spaces(act):
        for step in sorted(range(1, spaces), key=lambda step: -min(step, spaces - step)):
            act(lax.rem(here + step, spaces))

    def finish(buffer, count, semaphore):
        part = buffer.at[pl.ds(0, count)]
        pltpu.make_async_copy(part, part, semaphore).wait()

    barrier = pltpu.get_barrier_semaphore()

    near = (
        (me, nxt), (me, prv), (pair, here),
        (device_at(across + 1, along, core), here), (device_at(across + SIDE - 1, along, core), here),
        (device_at(across, along + 1, core), here), (device_at(across, along + SIDE - 1, core), here),
    )

    def greet(semaphore):
        for device in near:
            pl.semaphore_signal(semaphore, inc=1, device_id=device, device_id_type=MESH)

    def hand_on(k):
        if k > 0:
            pl.semaphore_wait(relay_sem.at[k - 1], len(near))
        if k < RELAYS:
            greet(relay_sem.at[k])

    greet(barrier)
    for load in loads:
        load.start()

    loads[0].wait()
    loads[1].wait()

    def spread(source, parity, plane):
        for first, start, count in ((0, LINES - 8, 8), (8, 0, LINES), (LINES + 8, 0, 8)):
            own[plane, pl.ds(first, count), :] = source[pl.ds(2 * start + parity, count, stride=2), :]

    def spread_field(f, carry):
        for r in range(2):
            spread(fields_ref.at[f], r, 1 + FIELDS * r + f)
        return carry

    lax.fori_loop(0, FIELDS, spread_field, 0)
    for r in range(2):
        spread(visc_ref, r, 9 * r)
    pl.semaphore_wait(barrier, len(near))

    def halo(n):
        lines = pl.ds(pl.multiple_of(BATCH * n, BATCH), BATCH)
        down = pltpu.make_async_remote_copy(
            src_ref=own.at[pl.ds(0, 9), lines], dst_ref=high.at[:, lines],
            send_sem=halo_send_sem.at[0, n], recv_sem=halo_recv_sem.at[0, n],
            device_id=(me, prv), device_id_type=MESH,
        )
        up = pltpu.make_async_remote_copy(
            src_ref=own.at[pl.ds(1, 9), lines], dst_ref=low.at[:, lines],
            send_sem=halo_send_sem.at[1, n], recv_sem=halo_recv_sem.at[1, n],
            device_id=(me, nxt), device_id_type=MESH,
        )
        return down, up

    def start_halo(n):
        for copy in halo(n):
            copy.start()

    start_halo(0)
    start_halo(1)
    hand_on(0)

    loads[2].wait()

    def fill_columns(k, carry):
        @pl.when(lax.rem(k, 8) == 0)
        def _():
            start_halo(2 + k // 8)

        rows = pl.ds(pl.multiple_of(256 * core + 8 * k, 8), 8)
        beam_col = (beam_ref[rows, :] & (BEAM_COLS - 1)).astype(F32).astype(BF16)
        ids = bf16_iota((BEAM_COLS, LANES), 0)
        ones, zeros = jnp.ones((BEAM_COLS, LANES), BF16), jnp.zeros((BEAM_COLS, LANES), BF16)
        for g in range(8):
            columns[k, g * LANES : (g + 1) * LANES, :] = jnp.where(
                ids == beam_col[g : g + 1], ones, zeros
            ).T
        return carry

    lax.fori_loop(0, 4 * BATCHES, fill_columns, 0)
    for load in loads[3:]:
        load.wait()

    def step_batch(n):
        lines = pl.ds(pl.multiple_of(BATCH * n, BATCH), 2 * BATCH)
        viscous = [low[8, lines], own[0, lines], own[9, lines], high[0, lines]]
        for group in ((2, 3), (0,), (1,)):
            rows = {
                f: [low[f, lines], low[4 + f, lines], own[1 + f, lines],
                    own[5 + f, lines], high[1 + f, lines], high[5 + f, lines]]
                for f in group
            }
            for depth in (4, 2):
                nu = viscous if depth == 4 else viscous[1:3]
                after = {
                    f: [
                        stencil(rows[f][i + 1], rows[f][i], rows[f][i + 2], nu[i])
                        for i in range(depth)
                    ]
                    for f in group
                }
                if len(group) == 2:
                    lift, heat = group
                    after[lift] = [
                        after[lift][i] + BUOYANCY * rows[heat][i + 1] for i in range(depth)
                    ]
                    after[heat] = [
                        after[heat][i] - BUOYANCY * rows[lift][i + 1] for i in range(depth)
                    ]
                rows = after
            for f in group:
                for r in range(2):
                    for h in range(2):
                        block = members // 2 * r + 2 * n + h
                        forecast[block, f] = rows[f][r][8 + 8 * h : 16 + 8 * h]

    def gather_batch(n):
        slot = lax.min(n, BATCHES)
        for r in range(2):
            for h in range(2):
                block = members // 2 * r + 2 * lax.min(n, BATCHES - 1) + h
                for g in range(2):
                    rows = pl.ds(pl.multiple_of(16 * block + 8 * g, 8), 8)
                    cells = cell_ref[rows, :]
                    lane, line = cells & (LANES - 1), cells >> 7
                    total = None
                    for c in range(3):
                        table = forecast[block, c]
                        value = None
                        for t in range(8):
                            row = jnp.broadcast_to(table[t : t + 1], (8, LANES))
                            found = jnp.take_along_axis(
                                row, lane, axis=1, mode="promise_in_bounds"
                            )
                            value = found if value is None else jnp.where(line == t, found, value)
                        term = weight_ref[c, rows, :] * value
                        total = term if total is None else total + term
                    sight[r, slot, 16 * h + 8 * g : 16 * h + 8 * g + 8, :] = total

    def pair_copy(n):
        return pltpu.make_async_remote_copy(
            src_ref=sight.at[1 - core, n], dst_ref=pair_sight.at[n],
            send_sem=sight_send_sem.at[n], recv_sem=sight_recv_sem.at[n],
            device_id=(pair, here), device_id_type=MESH,
        )

    def scatter_batch(n):
        ids = bf16_iota((BEAM_ROWS, LANES), 0)
        zeros = jnp.zeros((BEAM_ROWS, LANES), BF16)
        left = []
        for h in range(2):
            lines = slice(16 * h, 16 * h + 16)
            parts = split(sight[core, n, lines, :], PARTS) + split(pair_sight[n, lines, :], PARTS)
            rows = pl.ds(pl.multiple_of(256 * core + 32 * n + 16 * h, 16), 16)
            beam_row = (beam_ref[rows, :] >> 8).astype(F32).astype(BF16)
            for g in range(16):
                hit = ids == beam_row[g : g + 1]
                left.append(jnp.concatenate([
                    jnp.where(hit, jnp.broadcast_to(part[g : g + 1], (BEAM_ROWS, LANES)), zeros)
                    for part in parts
                ], axis=0))
        right = columns[pl.ds(4 * n, 4)].reshape(32 * LANES, BEAM_COLS)
        scatter[...] += jnp.dot(
            jnp.concatenate(left, axis=1), right, preferred_element_type=F32
        )

    def there(p):
        return pltpu.make_async_remote_copy(
            src_ref=forecast.at[p], dst_ref=pointwise.at[me],
            send_sem=there_send_sem, recv_sem=there_recv_sem,
            device_id=(p, here), device_id_type=MESH,
        )

    scatter[...] = jnp.zeros_like(scatter)

    def finish_halo(n):
        for copy in halo(n):
            copy.wait_recv()

    def send_blocks(n):
        for r in range(2):
            for h in range(2):
                block = members // 2 * r + 2 * n + h

                @pl.when(block != me)
                def _():
                    there(block).start()

    hand_on(1)
    finish_halo(0)
    for buffer in (low, high):
        buffer[:, LINES : LINES + BATCH, :] = buffer[:, 0:BATCH, :]

    def first_batch(n, carry):
        finish_halo(n + 1)
        start_halo(BATCHES - LAG + n)
        step_batch(n)
        gather_batch(n)
        pair_copy(n).start()
        for k in range(LAG):
            @pl.when(n == k)
            def _():
                hand_on(2 + k)

        return carry

    def batch(n, carry):
        @pl.when(n < BATCHES - 1)
        def _():
            finish_halo(n + 1)

        @pl.when(n < BATCHES)
        def _():
            step_batch(n)

        pair_copy(n - LAG).wait_recv()
        scatter_batch(n - LAG)
        gather_batch(n)

        @pl.when(n < BATCHES)
        def _():
            pair_copy(n).start()

        @pl.when(n == LAG)
        def _():
            hand_on(RELAYS)

        return carry

    lax.fori_loop(0, LAG, first_batch, 0)
    lax.fori_loop(LAG, BATCHES + LAG, batch, 0)
    for half in range(2):
        first = 2 * BEAM_ROWS * half
        total = scatter[first : first + BEAM_ROWS] + scatter[first + BEAM_ROWS : first + 2 * BEAM_ROWS]
        beam_send[pl.ds(spaces * half, spaces)] = total.reshape((spaces,) + beam_send.shape[1:])

    def beam_to(half, t):
        return pltpu.make_async_remote_copy(
            src_ref=beam_send.at[spaces * half + t], dst_ref=beam_recv.at[spaces * half + here],
            send_sem=beam_send_sem, recv_sem=beam_recv_sem,
            device_id=(pair if half else me, t), device_id_type=MESH,
        )

    def send_share(t):
        beam_to(0, t).start()
        beam_to(1, t).start()

    other_spaces(send_share)
    beam_to(1, here).start()
    beam_recv[here] = beam_send[here]
    other_members(lambda p: there(p).start(), 0, members // 2)
    pointwise[me] = forecast[me]
    finish(beam_recv, 2 * spaces - 1, beam_recv_sem)
    predicted = beam_recv[0] + beam_recv[spaces]
    for t in range(1, spaces):
        predicted = predicted + (beam_recv[t] + beam_recv[spaces + t])

    for half in range(2):
        share[half] = predicted[:, half * LANES : (half + 1) * LANES]

    def slot(i):
        return gathered.at[pl.ds(pl.multiple_of(8 * i, 8), 8), :]

    def share_to(p):
        return pltpu.make_async_remote_copy(
            src_ref=share.at[lax.rem(p, 2)], dst_ref=slot(me),
            send_sem=gather_send_sem, recv_sem=gather_recv_sem,
            device_id=(p, here), device_id_type=MESH,
        )

    other_members(lambda p: share_to(p).start())
    gathered[pl.ds(pl.multiple_of(8 * me, 8), 8), :] = share[core]
    finish(gathered, 8 * (members - 1), gather_recv_sem)

    every = jnp.concatenate(
        [gathered[pl.ds(sub, members, stride=8), :] for sub in range(8)], axis=1
    )
    mine = pl.ds(pl.multiple_of(16 * here, 16), 16)

    def core_rows(ref):
        rows = ref[mine, :]
        return jnp.concatenate([
            jnp.where(core == 0, rows[2 * i : 2 * i + 1], rows[2 * i + 1 : 2 * i + 2])
            for i in range(8)
        ], axis=1)

    seen, variance = core_rows(observed_ref), core_rows(variance_ref)
    mean_pred = jnp.mean(every, axis=0, keepdims=True)
    anomaly = every - mean_pred
    scaled = anomaly / variance
    member_id = lax.broadcasted_iota(jnp.int32, anomaly.shape, 0)
    against = jnp.where(member_id == members - 1, seen - mean_pred, anomaly)
    product = lax.dot_general(
        jnp.concatenate(split(scaled, 3), axis=0), jnp.concatenate(split(against, 3), axis=0),
        (((1,), (1,)), ((), ())), preferred_element_type=F32,
    )

    def term(i, j):
        return product[members * i : members * (i + 1), members * j : members * (j + 1)]

    partial = term(0, 0) + ((term(0, 1) + term(1, 0)) + (term(1, 1) + (term(0, 2) + term(2, 0))))
    stats_send[...] = jnp.concatenate([partial[8 * g : 8 * g + 8] for g in range(members // 8)], axis=1)

    def stats_to(other, t):
        return pltpu.make_async_remote_copy(
            src_ref=stats_send, dst_ref=stats_recv.at[spaces * core + here],
            send_sem=stats_send_sem, recv_sem=stats_recv_sem,
            device_id=(pair if other else me, t), device_id_type=MESH,
        )

    def send_stats(t):
        stats_to(0, t).start()
        stats_to(1, t).start()

    other_spaces(send_stats)
    stats_to(1, here).start()
    other_members(lambda p: there(p).start(), members // 2)
    stats_recv[spaces * core + here] = stats_send[...]
    finish(stats_recv, 2 * spaces - 1, stats_recv_sem)
    packed = stats_recv[0] + stats_recv[spaces]
    for t in range(1, spaces):
        packed = packed + (stats_recv[t] + stats_recv[spaces + t])
    stats = jnp.concatenate(
        [packed[:, members * g : members * (g + 1)] for g in range(members // 8)], axis=0
    )

    row_id = lax.broadcasted_iota(jnp.int32, (members, members), 0)
    col_id = lax.broadcasted_iota(jnp.int32, (members, members), 1)
    last = col_id == members - 1
    rest = jnp.sum(jnp.where(last, 0.0, stats), axis=1, keepdims=True)
    covar = jnp.where(last, -rest, stats)
    identity = jnp.where(row_id == col_id, 1.0, 0.0).astype(F32)
    system = identity + covar / (members - 1.0)
    magnitude = jnp.sqrt(jnp.sum(system * system, axis=(0, 1), keepdims=True))
    iterate = system / magnitude

    def newton(_, pair_of):
        iterate, inverse_root = pair_of
        factor = 1.5 * identity - 0.5 * times(inverse_root, iterate)
        return times(iterate, factor), times(factor, inverse_root)

    factor = 1.5 * identity - 0.5 * iterate
    _, inverse_root = lax.fori_loop(1, NS_STEPS, newton, (times(iterate, factor), factor))
    root_part = inverse_root / jnp.sqrt(magnitude)
    inverse_full = times(inverse_root, inverse_root) / magnitude
    shift = times(inverse_full, stats)[:, members - 1 : members] / (members - 1.0)
    combined = root_part + shift
    mixing = combined - jnp.mean(combined, axis=0, keepdims=True) + 1.0 / members
    mixing_ref[...] = mixing

    finish(pointwise, members - 1, there_recv_sem)
    count = FIELDS * 8
    sources, targets = (ref.reshape(members * count, LANES) for ref in (pointwise, mixed))
    mix0, mix1 = split(mixing, 2)
    weights = jnp.concatenate([mix0, mix1, mix0, mix1], axis=0)

    def mix_field(f, carry):
        def lines(k):
            return pl.ds(8 * f + k, members, stride=count)

        block = jnp.concatenate([sources[lines(k), :] for k in range(8)], axis=1)
        block0, block1 = split(block, 2)
        analysed = lax.dot_general(
            weights, jnp.concatenate([block0, block0, block1, block1], axis=0),
            (((0,), (0,)), ((), ())), preferred_element_type=F32,
        )
        for k in range(8):
            targets[lines(k), :] = analysed[:, k * LANES : (k + 1) * LANES]
        return carry

    lax.fori_loop(0, FIELDS, mix_field, 0)

    def back(j):
        return pltpu.make_async_remote_copy(
            src_ref=mixed.at[j], dst_ref=returned.at[me],
            send_sem=back_send_sem, recv_sem=back_recv_sem,
            device_id=(j, here), device_id_type=MESH,
        )

    other_members(lambda j: back(j).start())
    returned[me] = mixed[me]

    def finish_send(n, carry):
        for copy in halo(n):
            copy.wait_send()
        pair_copy(n).wait_send()
        return carry

    lax.fori_loop(0, BATCHES, finish_send, 0)
    finish(forecast, members - 1, there_send_sem)
    finish(beam_send, 2 * spaces - 1, beam_send_sem)
    finish(stats_recv, 2 * spaces - 1, stats_send_sem)
    finish(gathered, 8 * (members - 1), gather_send_sem)
    finish(returned, members - 1, back_recv_sem)
    stores = [
        pltpu.make_async_copy(out_ref.at[f], out_hbm.at[f], store_sem.at[f]) for f in range(FIELDS)
    ]
    for f in range(FIELDS):
        for p in range(members):
            r, q = divmod(p, members // 2)
            out_ref[f, pl.ds(16 * q + r, 8, stride=2), :] = returned[p, f]
        stores[f].start()
    for store in stores:
        store.wait()
    finish(mixed, members - 1, back_send_sem)


def shards(members, spaces, realization_fields, viscosity, cell_index, beam_id, los_weight, observed, obs_variance):
    _, fields, rows, plane = realization_fields.shape
    lines = plane // LANES
    samples = cell_index.shape[1] // LANES
    beams = observed.shape[0] // LANES
    mixed_rows = realization_fields.reshape(fields, rows, lines, LANES).transpose(0, 2, 1, 3)
    visc_rows = viscosity.reshape(rows, lines, LANES).transpose(1, 0, 2)
    block = (members, FIELDS, 8, LANES)
    share = (BEAM_ROWS // spaces, BEAM_COLS)
    dma = lambda *shape: pltpu.SemaphoreType.DMA(shape)
    vmem = pl.BlockSpec(memory_space=pltpu.VMEM)
    analysis, mixing = pl.pallas_call(
        functools.partial(kernel, members, spaces),
        out_shape=(
            jax.ShapeDtypeStruct((fields, rows * lines, LANES), F32),
            jax.ShapeDtypeStruct((members, members), F32),
        ),
        in_specs=[pl.BlockSpec(memory_space=pl.ANY)] * 7,
        out_specs=(pl.BlockSpec(memory_space=pl.ANY), vmem),
        scratch_shapes=[
            pltpu.VMEM((fields, rows * lines, LANES), F32),
            pltpu.VMEM((fields, rows * lines, LANES), F32),
            pltpu.VMEM((rows * lines, LANES), F32),
            pltpu.VMEM((samples, LANES), jnp.int32),
            pltpu.VMEM((samples, LANES), jnp.int32),
            pltpu.VMEM((3, samples, LANES), F32),
            pltpu.VMEM((beams, LANES), F32),
            pltpu.VMEM((beams, LANES), F32),
            pltpu.VMEM((10, LINES + BATCH, LANES), F32),
            pltpu.VMEM((9, LINES + BATCH, LANES), F32),
            pltpu.VMEM((9, LINES + BATCH, LANES), F32),
            pltpu.VMEM(block, F32),
            pltpu.VMEM(block, F32),
            pltpu.VMEM((2, BATCHES + 1, 32, LANES), F32),
            pltpu.VMEM((BATCHES, 32, LANES), F32),
            pltpu.VMEM((4 * BATCHES, 8 * LANES, BEAM_COLS), BF16),
            pltpu.VMEM((2 * PARTS * BEAM_ROWS, BEAM_COLS), F32),
            pltpu.VMEM((2 * spaces,) + share, F32),
            pltpu.VMEM((2 * spaces,) + share, F32),
            pltpu.VMEM((2, share[0], LANES), F32),
            pltpu.VMEM((members * share[0], LANES), F32),
            pltpu.VMEM((8, LANES), F32),
            pltpu.VMEM((2 * spaces, 8, LANES), F32),
            pltpu.VMEM(block, F32),
            pltpu.VMEM(block, F32),
            dma(7), dma(fields), pltpu.SemaphoreType.REGULAR((RELAYS,)),
            dma(2, BATCHES), dma(2, BATCHES),
            dma(BATCHES), dma(BATCHES),
            *([pltpu.SemaphoreType.DMA] * 10),
        ],
        compiler_params=pltpu.CompilerParams(
            collective_id=0, has_side_effects=True, vmem_limit_bytes=60 << 20
        ),
    )(
        mixed_rows.reshape(fields, lines * rows, LANES),
        visc_rows.reshape(lines * rows, LANES),
        cell_index.reshape(samples, LANES),
        beam_id.reshape(samples, LANES),
        los_weight.reshape(3, samples, LANES),
        observed.reshape(beams, LANES),
        obs_variance.reshape(beams, LANES),
    )
    analysis = analysis.reshape(fields, lines, rows, LANES).transpose(0, 2, 1, 3)
    return analysis.reshape(realization_fields.shape), mixing


def solution(mesh):
    return jax.shard_map(
        functools.partial(shards, mesh.shape["member"], mesh.shape["space"]),
        mesh=mesh,
        in_specs=(
            P("member", None, "space", None),
            P("space", None),
            P("space", None),
            P("space", None),
            P("space", None, None),
            P(),
            P(),
        ),
        out_specs=(P("member", None, "space", None), P()),
        check_vma=False,
    )
```
